32 devices in a mesh: dp: 8 (over y, x, core), seq: 4 (over z).
Axes of the slice: x: 2, y: 2, z: 4, core: 2. Of those that a mesh axis runs over, the one named last changes fastest.
Arguments:
- tokens: bfloat16 [16, 2048, 576], P('dp', 'seq'), may hold values from -54 to 54
- positions: int32 [16, 2048], P('dp', 'seq'), may hold values from 0 to 2047, as said below
- cotangent: bfloat16 [16, 2048, 576], P('dp', 'seq'), may hold values from -6 to 6
- balance: float32 [576], P('seq'), may hold values from 0.5 to 1.5
- projector: float32 [576, 960], P('seq'), may hold values from -0.25 to 0.25
- combiner: float32 [576, 576], P('seq'), may hold values from -4 to 4
- leveler: float32 [576], P('seq'), may hold values from 0.5 to 1.5
- expander: float32 [576, 3072], P('seq'), may hold values from -0.25 to 0.25
- reducer: float32 [1536, 576], P('seq'), may hold values from -0.15625 to 0.15625
- mean_balance: float32 [576], P('seq'), may hold values from -724.07733 to 724.07733
- mean_projector: float32 [576, 960], P('seq'), may hold values from -325.8348 to 325.8348
- mean_combiner: float32 [576, 576], P('seq'), may hold values from -11.2 to 11.2
- mean_leveler: float32 [576], P('seq'), may hold values from -162.9174 to 162.9174
- mean_expander: float32 [576, 3072], P('seq'), may hold values from -119.47276 to 119.47276
- mean_reducer: float32 [1536, 576], P('seq'), may hold values from -119.47276 to 119.47276
- square_balance: float32 [576], P('seq'), may hold values from 6553.6 to 104857.6
- square_projector: float32 [576, 960], P('seq'), may hold values from 1310.72 to 20971.52
- square_combiner: float32 [576, 576], P('seq'), may hold values from 1.6 to 25.6
- square_leveler: float32 [576], P('seq'), may hold values from 327.68 to 5242.88
- square_expander: float32 [576, 3072], P('seq'), may hold values from 163.84 to 2621.44
- square_reducer: float32 [1536, 576], P('seq'), may hold values from 163.84 to 2621.44
Outputs:
- layer_out: bfloat16 [16, 2048, 576], P('dp', 'seq')
- tokens_grad: bfloat16 [16, 2048, 576], P('dp', 'seq')
- grad_balance: float32 [576], P('seq')
- grad_projector: float32 [576, 960], P('seq')
- grad_combiner: float32 [576, 576], P('seq')
- grad_leveler: float32 [576], P('seq')
- grad_expander: float32 [576, 3072], P('seq')
- grad_reducer: float32 [1536, 576], P('seq')
- next_balance: float32 [576], P('seq')
- next_projector: float32 [576, 960], P('seq')
- next_combiner: float32 [576, 576], P('seq')
- next_leveler: float32 [576], P('seq')
- next_expander: float32 [576, 3072], P('seq')
- next_reducer: float32 [1536, 576], P('seq')
- newmean_balance: float32 [576], P('seq')
- newmean_projector: float32 [576, 960], P('seq')
- newmean_combiner: float32 [576, 576], P('seq')
- newmean_leveler: float32 [576], P('seq')
- newmean_expander: float32 [576, 3072], P('seq')
- newmean_reducer: float32 [1536, 576], P('seq')
- newsquare_balance: float32 [576], P('seq')
- newsquare_projector: float32 [576, 960], P('seq')
- newsquare_combiner: float32 [576, 576], P('seq')
- newsquare_leveler: float32 [576], P('seq')
- newsquare_expander: float32 [576, 3072], P('seq')
- newsquare_reducer: float32 [1536, 576], P('seq')
The draws below stay inside these ranges and needn't reach their ends.
Inputs may be any that keep to these rules, and one draw needn't show every extreme that they name: `positions`: in every sequence the first token has position 0, and each later token has either position 0 (a new document begins) or its predecessor's position plus 1; the first sequence is one whole document.
All inputs are finite; a program needn't handle non-finite values.
Results may differ from the reference program's by a relative error of at most 0.025.
Values may be sent and summed in bfloat16 or wider, within the bound.
A program may use at most 448 MiB of HBM per device.

```python
import math
import jax
import jax.numpy as jnp
from jax import lax

D = 576
HEADS = 9
KV_HEADS = 3
HEAD_DIM = 64
FF = 1536
LENGTH = 2048
STEP = 2
SEQUENCES = 16
INNER = 576
QKV = 960


def draw_tokens(key, part):
    keys_all = jax.random.split(key, 3)
    shape_all = (SEQUENCES, LENGTH, D)
    base = jnp.clip(jax.random.normal(keys_all[0], shape_all, jnp.float32), -6.0, 6.0)
    row_scale = jnp.exp(jax.random.uniform(keys_all[1], (SEQUENCES, LENGTH, 1), jnp.float32, math.log(0.3), math.log(3.0)))
    col_scale = jnp.exp(jax.random.uniform(keys_all[2], (1, 1, D), jnp.float32, math.log(0.3), math.log(3.0)))
    return (base * row_scale * col_scale).astype(jnp.bfloat16)


def draw_positions(key, part):
    flags = jax.random.randint(key, (SEQUENCES, LENGTH), 0, LENGTH) < 3
    index = jnp.arange(LENGTH, dtype=jnp.int32)[None, :]
    seq_number = jnp.arange(SEQUENCES, dtype=jnp.int32)[:, None]
    flags = flags & (seq_number > 0) | (index == 0)
    starts = jnp.where(flags, index, 0).astype(jnp.int32)
    starts = lax.cummax(starts, axis=1)
    return (index - starts).astype(jnp.int32)


def block_scale(stream_key, extent, cuts, smallest, top_value):
    def one(position, blocks):
        heights = jax.random.uniform(jax.random.fold_in(jax.random.fold_in(stream_key, 6), position), (blocks,), jnp.float32, smallest / len(cuts), top_value / len(cuts))
        return jnp.repeat(jnp.exp(heights), extent[position] // blocks).reshape((-1,) + (1,) * (len(extent) - position - 1))

    loudness = one(*cuts[0])
    for cut in cuts[1:]:
        loudness = loudness * one(*cut)
    return loudness


def normal_values(rng, extent, scale, bound, cuts=(), kind=jnp.bfloat16):
    entries = jax.random.normal(rng, extent, jnp.float32) * scale
    if len(cuts) > 0:
        entries = block_scale(rng, extent, cuts, -0.22, 0.18) * entries
    return jnp.clip(entries, min=-bound, max=bound).astype(kind)


def setup_inputs(seed: int = 0) -> dict:
    seeds = jax.random.split(jax.random.key(seed), 22)
    return {
        "tokens": draw_tokens(jax.random.fold_in(seeds[21], 71), 0),
        "positions": draw_positions(jax.random.fold_in(seeds[21], 71), 0),
        "cotangent": normal_values(seeds[2], (SEQUENCES, LENGTH, D), 1.0, 6.0, ((0, 8), (1, 4))),
        "balance": jnp.clip(1.0 + 0.1 * jax.random.normal(seeds[3], (D,), jnp.float32), 0.5, 1.5),
        "projector": normal_values(seeds[4], (D, QKV), D ** -0.5, 0.25, ((0, 4),), jnp.float32),
        "combiner": normal_values(seeds[5], (INNER, D), (max(INNER // 256, 1)) ** -0.5, 4.0, ((0, 4),), jnp.float32),
        "leveler": jnp.clip(1.0 + 0.1 * jax.random.normal(seeds[6], (D,), jnp.float32), 0.5, 1.5),
        "expander": normal_values(seeds[7], (D, 2 * FF), D ** -0.5, 0.25, ((0, 4),), jnp.float32),
        "reducer": normal_values(seeds[8], (FF, D), FF ** -0.5, 0.15625, ((0, 4),), jnp.float32),
        "mean_balance": normal_values(seeds[9], (D,), (0.67 * (SEQUENCES * LENGTH) ** 0.5), 724.07733, ((0, 4),), jnp.float32),
        "mean_projector": normal_values(seeds[10], (D, QKV), (0.3 * (SEQUENCES * LENGTH) ** 0.5), 325.8348, ((0, 4),), jnp.float32),
        "mean_combiner": normal_values(seeds[11], (INNER, D), (0.47 * SEQUENCES ** 0.5), 11.2, ((0, 4),), jnp.float32),
        "mean_leveler": normal_values(seeds[12], (D,), (0.15 * (SEQUENCES * LENGTH) ** 0.5), 162.9174, ((0, 4),), jnp.float32),
        "mean_expander": normal_values(seeds[13], (D, 2 * FF), (0.11 * (SEQUENCES * LENGTH) ** 0.5), 119.47276, ((0, 4),), jnp.float32),
        "mean_reducer": normal_values(seeds[14], (FF, D), (0.11 * (SEQUENCES * LENGTH) ** 0.5), 119.47276, ((0, 4),), jnp.float32),
        "square_balance": jnp.clip(jnp.exp(math.log(104857.6) - 2.7725887 * jax.random.uniform(seeds[15], (D,), jnp.float32) ** block_scale(seeds[15], (D,), ((0, 4),), -0.2, 0.2)), 6553.6, 104857.6),
        "square_projector": jnp.clip(jnp.exp(math.log(20971.52) - 2.7725887 * jax.random.uniform(seeds[16], (D, QKV), jnp.float32) ** block_scale(seeds[16], (D, QKV), ((0, 4),), -0.2, 0.2)), 1310.72, 20971.52),
        "square_combiner": jnp.clip(jnp.exp(math.log(25.6) - 2.7725887 * jax.random.uniform(seeds[17], (INNER, D), jnp.float32) ** block_scale(seeds[17], (INNER, D), ((0, 4),), -0.2, 0.2)), 1.6, 25.6),
        "square_leveler": jnp.clip(jnp.exp(math.log(5242.88) - 2.7725887 * jax.random.uniform(seeds[18], (D,), jnp.float32) ** block_scale(seeds[18], (D,), ((0, 4),), -0.2, 0.2)), 327.68, 5242.88),
        "square_expander": jnp.clip(jnp.exp(math.log(2621.44) - 2.7725887 * jax.random.uniform(seeds[19], (D, 2 * FF), jnp.float32) ** block_scale(seeds[19], (D, 2 * FF), ((0, 4),), -0.2, 0.2)), 163.84, 2621.44),
        "square_reducer": jnp.clip(jnp.exp(math.log(2621.44) - 2.7725887 * jax.random.uniform(seeds[20], (FF, D), jnp.float32) ** block_scale(seeds[20], (FF, D), ((0, 4),), -0.2, 0.2)), 163.84, 2621.44),
    }


@jax.custom_vjp
def low(v):
    return lax.optimization_barrier(v.astype(jnp.bfloat16)).astype(jnp.float32)

@jax.custom_vjp
def low_back(v):
    return v

def low_keep(v):
    return (low(v), None)

def low_pass(kept, grad):
    return (grad,)

def back_keep(v):
    return (v, None)

def back_low(kept, grad):
    return (low(grad),)
low.defvjp(low_keep, low_pass)
low_back.defvjp(back_keep, back_low)
norm_eps = 1e-05
rope_base = 100000.0
beta_one = 0.9
beta_two = 0.95
adam_eps = 1e-08
learn_rate = 0.2
decay_rate = 0.1
highest = lax.Precision.HIGHEST

def rms_scale(values, scales):
    factor = lax.rsqrt(lax.optimization_barrier(jnp.mean(values * values, axis=-1, keepdims=True)) + norm_eps)
    return values * factor * scales

def angles(token_pos):
    exponent = jnp.arange(HEAD_DIM // 2, dtype=jnp.float32) * (2.0 / HEAD_DIM)
    inverse = jnp.power(rope_base, -exponent)
    return token_pos.astype(jnp.float32)[..., None] * inverse

def rotate(values, phases):
    half_dim = values.shape[-1] // 2
    first = values[..., :half_dim]
    second = values[..., half_dim:]
    cosine = jnp.cos(phases)[..., None, :]
    sine_part = jnp.sin(phases)[..., None, :]
    return jnp.concatenate([first * cosine - second * sine_part, second * cosine + first * sine_part], axis=-1)

def one_sequence(weights, seq_tokens, seq_positions):
    gain_one, proj_in, comb_out, gain_two, expand_w, shrink_w = weights
    inner_width = HEADS * HEAD_DIM
    kv_width = KV_HEADS * HEAD_DIM
    group_size = HEADS // KV_HEADS
    normed = low(rms_scale(seq_tokens, gain_one))
    projected = low_back(jnp.dot(normed, proj_in, precision=highest))
    phases = angles(seq_positions)
    queries = low(rotate(projected[:, :inner_width].reshape(LENGTH, HEADS, HEAD_DIM), phases))
    keys_rot = low(rotate(projected[:, inner_width:inner_width + kv_width].reshape(LENGTH, KV_HEADS, HEAD_DIM), phases))
    values_in = low(projected[:, inner_width + kv_width:].reshape(LENGTH, KV_HEADS, HEAD_DIM))
    keys_full = jnp.repeat(keys_rot, group_size, axis=1)
    values_full = jnp.repeat(values_in, group_size, axis=1)
    scores = low_back(0.125 * jnp.einsum('qhd,khd->hqk', queries, keys_full, precision=highest))
    index = jnp.arange(LENGTH, dtype=jnp.int32)
    lowest = index - seq_positions.astype(jnp.int32)
    visible = (index[None, :] <= index[:, None]) & (index[None, :] >= lowest[:, None])
    masked = jnp.where(visible[None], scores, -1e+30)
    totals = jax.nn.logsumexp(masked, axis=-1, keepdims=True)
    weights_att = jnp.where(visible[None], jnp.exp(masked - totals), 0.0)
    mixed = jnp.einsum('hqk,khd->qhd', low(weights_att), values_full, precision=highest)
    heads_out = low_back(low(mixed.reshape(LENGTH, inner_width)))
    middle = seq_tokens + low_back(jnp.dot(heads_out, comb_out, precision=highest))
    normed_two = low(rms_scale(middle, gain_two))
    gate_up = low_back(jnp.dot(normed_two, expand_w, precision=highest))
    active = low(jax.nn.silu(gate_up[:, :FF]) * gate_up[:, FF:])
    return middle + low_back(jnp.dot(active, shrink_w, precision=highest))

def adam_step(master, grad_total, mean_old, square_old, decays):
    mean_new = beta_one * mean_old + (1.0 - beta_one) * grad_total
    square_new = beta_two * square_old + (1.0 - beta_two) * grad_total * grad_total
    mean_hat = mean_new / (1.0 - beta_one ** STEP)
    square_hat = square_new / (1.0 - beta_two ** STEP)
    change = mean_hat / (jnp.sqrt(square_hat) + adam_eps)
    if decays:
        change = change + decay_rate * master
    return (master - learn_rate * change, mean_new, square_new)

def reference(tokens, positions, cotangent, balance, projector, combiner, leveler, expander, reducer, mean_balance, mean_projector, mean_combiner, mean_leveler, mean_expander, mean_reducer, square_balance, square_projector, square_combiner, square_leveler, square_expander, square_reducer):

    def forward(tokens_f, masters):
        weights = tuple((low(master) for master in masters))

        def per_sequence(seq_item):
            return one_sequence(weights, seq_item[0], seq_item[1])
        return lax.map(jax.checkpoint(per_sequence), (tokens_f, positions))
    masters = (balance, projector, combiner, leveler, expander, reducer)
    layer_out, pullback = jax.vjp(forward, tokens.astype(jnp.float32), masters)
    tokens_grad, grads = pullback(cotangent.astype(jnp.float32))
    means = (mean_balance, mean_projector, mean_combiner, mean_leveler, mean_expander, mean_reducer)
    squares = (square_balance, square_projector, square_combiner, square_leveler, square_expander, square_reducer)
    decay_flags = (False, True, True, False, True, True)
    results = [adam_step(masters[number], grads[number], means[number], squares[number], decay_flags[number]) for number in range(6)]
    return (layer_out.astype(jnp.bfloat16), tokens_grad.astype(jnp.bfloat16), grads[0], grads[1], grads[2], grads[3], grads[4], grads[5], results[0][0], results[1][0], results[2][0], results[3][0], results[4][0], results[5][0], results[0][1], results[1][1], results[2][1], results[3][1], results[4][1], results[5][1], results[0][2], results[1][2], results[2][2], results[3][2], results[4][2], results[5][2])
```

```python
import functools

import jax
import jax.numpy as jnp
from jax import lax
from jax.experimental import pallas as pl
from jax.experimental.pallas import tpu as pltpu
from jax.sharding import PartitionSpec as P

HEADS = 9
KV_HEADS = 3
HEAD_DIM = 64
HALF = HEAD_DIM // 2
GROUP = HEADS // KV_HEADS
STEP = 2

norm_eps = 1e-05
rope_base = 100000.0
beta_one = 0.9
beta_two = 0.95
adam_eps = 1e-08
learn_rate = 0.2
decay_rate = 0.1

bf16 = jnp.bfloat16
f32 = jnp.float32
NEG = -1e30
NN = (((1,), (0,)), ((), ()))
NT = (((1,), (1,)), ((), ()))
MESH = pl.DeviceIdType.MESH
VMEM = pl.BlockSpec(memory_space=pltpu.VMEM)
HBM = pl.BlockSpec(memory_space=pl.ANY)


def dot(left, right, dims=NN):
    return lax.dot_general(left, right, dims, preferred_element_type=f32)


def place():
    dp = lax.axis_index("dp")
    base = (dp // 8) * 8
    chip = (dp % 8) // 2
    core = dp % 2
    return base, chip, core, lax.axis_index("seq")


def gather_kernel(count, blocks, *refs):
    quarters = refs[:count]
    fulls = refs[count : 2 * count]
    local_sem, send_sem, recv_sem = refs[2 * count :]
    base, chip, core, z = place()

    def window(number, which, quarter):
        kind, size, rows = blocks[number]
        if kind == "cols":
            return (
                pl.ds(pl.multiple_of(quarter * rows, 16), rows),
                pl.ds(pl.multiple_of(which * size, 128), size),
            )
        return (pl.ds(pl.multiple_of(quarter * rows + which * size, 16), size), slice(None))

    def dev(p, c, zz):
        return {"dp": base + 2 * p + c, "seq": zz}

    barrier = pltpu.get_barrier_semaphore()
    for r in range(1, 4):
        pl.semaphore_signal(
            barrier, inc=1, device_id=dev(chip, core, (z + r) % 4), device_id_type=MESH
        )
        pl.semaphore_signal(
            barrier, inc=1, device_id=dev((chip + r) % 4, core, z), device_id_type=MESH
        )
    pl.semaphore_signal(barrier, inc=1, device_id=dev(chip, 1 - core, z), device_id_type=MESH)
    pl.semaphore_wait(barrier, 7)

    def copy(number, src, dst, slot, target):
        return pltpu.make_async_remote_copy(
            src_ref=src,
            dst_ref=dst,
            send_sem=send_sem.at[number, slot],
            recv_sem=recv_sem.at[number, slot],
            device_id=target,
            device_id_type=MESH,
        )

    mine = 2 * chip + core
    started = []
    for number in range(count):
        for r in range(1, 4):
            started.append(
                copy(
                    number,
                    quarters[number].at[window(number, mine, 0)],
                    fulls[number].at[window(number, mine, z)],
                    r - 1,
                    dev(chip, core, (z + r) % 4),
                )
            )
            started[-1].start()
    locals_ = []
    for number in range(count):
        rows = quarters[number].shape[0]
        own = pltpu.make_async_copy(
            quarters[number],
            fulls[number].at[pl.ds(pl.multiple_of(z * rows, 16), rows), :],
            local_sem.at[number],
        )
        own.start()
        locals_.append(own)

    def landed(number, which, quarter, slot):
        ref = fulls[number].at[window(number, which, quarter)]
        return copy(number, ref, ref, slot, dev(chip, 1 - core, z))

    for number in range(count):
        for r in range(1, 4):
            quarter = (z + 4 - r) % 4
            landed(number, mine, quarter, r - 1).wait_recv()
            ref = fulls[number].at[window(number, mine, quarter)]
            for s in range(1, 4):
                started.append(
                    copy(number, ref, ref, 3 + 3 * (r - 1) + s - 1, dev((chip + s) % 4, core, z))
                )
                started[-1].start()
            started.append(copy(number, ref, ref, 12 + r - 1, dev(chip, 1 - core, z)))
            started[-1].start()
    for number in range(count):
        for r in range(1, 4):
            quarter = (z + 4 - r) % 4
            for s in range(1, 4):
                which = 2 * ((chip + 4 - s) % 4) + core
                landed(number, which, quarter, 3 + 3 * (r - 1) + s - 1).wait_recv()
                ref = fulls[number].at[window(number, which, quarter)]
                started.append(
                    copy(number, ref, ref, 15 + 3 * (r - 1) + s - 1, dev(chip, 1 - core, z))
                )
                started[-1].start()
    for number in range(count):
        for r in range(1, 4):
            quarter = (z + 4 - r) % 4
            landed(number, 2 * chip + 1 - core, quarter, 12 + r - 1).wait_recv()
            for s in range(1, 4):
                which = 2 * ((chip + 4 - s) % 4) + 1 - core
                landed(number, which, quarter, 15 + 3 * (r - 1) + s - 1).wait_recv()
    for item in started:
        item.wait_send()
    for item in locals_:
        item.wait()


def block_kind(array, row_blocks):
    if row_blocks:
        return ("rows", array.shape[0] // 8, array.shape[0])
    return ("cols", array.shape[1] // 8, array.shape[0])


def gather_weights(arrays, by_rows, collective):
    count = len(arrays)
    blocks = tuple(block_kind(a, r) for a, r in zip(arrays, by_rows))
    return pl.pallas_call(
        functools.partial(gather_kernel, count, blocks),
        out_shape=[jax.ShapeDtypeStruct((4 * a.shape[0], a.shape[1]), bf16) for a in arrays],
        in_specs=[HBM] * count,
        out_specs=[HBM] * count,
        scratch_shapes=[
            pltpu.SemaphoreType.DMA((count,)),
            pltpu.SemaphoreType.DMA((count, 24)),
            pltpu.SemaphoreType.DMA((count, 24)),
        ],
        compiler_params=pltpu.CompilerParams(collective_id=collective, has_side_effects=True),
    )(*arrays)


def scatter_kernel(count, blocks, *refs):
    grads = refs[:count]
    outs = refs[count : 2 * count]
    rest = refs[2 * count :]
    r0s = rest[:count]
    s0s = rest[count : 2 * count]
    r1s = rest[2 * count : 3 * count]
    r2s = rest[3 * count : 4 * count]
    send_sem, recv_sem = rest[4 * count :]
    base, chip, core, z = place()

    def dev(p, c, zz):
        return {"dp": base + 2 * p + c, "seq": zz}

    barrier = pltpu.get_barrier_semaphore()
    for r in range(1, 4):
        pl.semaphore_signal(
            barrier, inc=1, device_id=dev(chip, core, (z + r) % 4), device_id_type=MESH
        )
        pl.semaphore_signal(
            barrier, inc=1, device_id=dev((chip + r) % 4, core, z), device_id_type=MESH
        )
    pl.semaphore_signal(barrier, inc=1, device_id=dev(chip, 1 - core, z), device_id_type=MESH)
    pl.semaphore_wait(barrier, 7)

    started = []

    def copy(number, src, dst, slot, target):
        return pltpu.make_async_remote_copy(
            src_ref=src,
            dst_ref=dst,
            send_sem=send_sem.at[number, slot],
            recv_sem=recv_sem.at[number, slot],
            device_id=target,
            device_id_type=MESH,
        )

    def send(number, src, dst, slot, target):
        item = copy(number, src, dst, slot, target)
        item.start()
        started.append(item)

    def await_(number, ref, slot):
        copy(number, ref, ref, slot, dev(chip, 1 - core, z)).wait_recv()

    def block_of(number, which):
        kind, size, rows = blocks[number]
        if kind == "cols":
            return (slice(None), slice(None), pl.ds(pl.multiple_of(which * size, 128), size))
        return (slice(None), pl.ds(pl.multiple_of(which * size, 16), size), slice(None))

    def out_block(number, which):
        return block_of(number, which)[1:]

    for number in range(count):
        for s in range(4):
            p = (chip + s) % 4
            send(
                number,
                grads[number].at[block_of(number, 2 * p + 1 - core)],
                r0s[number].at[s],
                s,
                dev(chip, 1 - core, z),
            )
    for number in range(count):
        for s in (1, 2, 3, 0):
            p = (chip + s) % 4
            await_(number, r0s[number].at[s], s)
            total = (
                grads[number][block_of(number, 2 * p + core)].astype(f32)
                + r0s[number][s].astype(f32)
            )
            s0s[number][s] = total.astype(bf16)
            if s > 0:
                send(
                    number, s0s[number].at[s], r1s[number].at[s - 1], 3 + s, dev(p, core, z)
                )
    for number in range(count):
        total = s0s[number][0].astype(f32)
        for s in range(1, 4):
            await_(number, r1s[number].at[s - 1], 3 + s)
            total = total + r1s[number][s - 1].astype(f32)
        s0s[number][0] = total.astype(bf16)
        for r in range(1, 4):
            send(
                number,
                s0s[number].at[0, (z + r) % 4],
                r2s[number].at[r - 1],
                6 + r,
                dev(chip, core, (z + r) % 4),
            )
    mine = 2 * chip + core
    for number in range(count):
        total = s0s[number][0, z].astype(f32)
        for r in range(1, 4):
            await_(number, r2s[number].at[r - 1], 6 + r)
            total = total + r2s[number][r - 1].astype(f32)
        ref = outs[number].at[out_block(number, mine)]
        outs[number][out_block(number, mine)] = total.astype(bf16)
        for s in range(1, 4):
            send(number, ref, ref, 9 + s, dev((chip + s) % 4, core, z))
        send(number, ref, ref, 13, dev(chip, 1 - core, z))
    for number in range(count):
        for s in range(1, 4):
            which = 2 * ((chip + 4 - s) % 4) + core
            ref = outs[number].at[out_block(number, which)]
            await_(number, ref, 9 + s)
            send(number, ref, ref, 13 + s, dev(chip, 1 - core, z))
    for number in range(count):
        await_(number, outs[number].at[out_block(number, 2 * chip + 1 - core)], 13)
        for s in range(1, 4):
            which = 2 * ((chip + 4 - s) % 4) + 1 - core
            await_(number, outs[number].at[out_block(number, which)], 13 + s)
    for item in started:
        item.wait_send()


def scatter_grads(arrays, by_rows, collective):
    count = len(arrays)
    split = [a.reshape(4, a.shape[0] // 4, a.shape[1]) for a in arrays]
    blocks = tuple(block_kind(a[0], r) for a, r in zip(split, by_rows))
    parts = []
    for array, (kind, size, rows) in zip(split, blocks):
        parts.append((4, rows, size) if kind == "cols" else (4, size, array.shape[2]))
    scratch = (
        [pltpu.VMEM((4,) + part, bf16) for part in parts]
        + [pltpu.VMEM((4,) + part, bf16) for part in parts]
        + [pltpu.VMEM((3,) + part, bf16) for part in parts]
        + [pltpu.VMEM((3,) + part[1:], bf16) for part in parts]
    )
    return pl.pallas_call(
        functools.partial(scatter_kernel, count, blocks),
        out_shape=[jax.ShapeDtypeStruct(a.shape[1:], bf16) for a in split],
        in_specs=[VMEM] * count,
        out_specs=[VMEM] * count,
        scratch_shapes=scratch
        + [pltpu.SemaphoreType.DMA((count, 17)), pltpu.SemaphoreType.DMA((count, 17))],
        compiler_params=pltpu.CompilerParams(
            collective_id=collective, has_side_effects=True, vmem_limit_bytes=60 << 20
        ),
    )(*split)


def column_row(tile, lane, height):
    return tile.astype(f32).T[lane : lane + 1, :]


def qkv_kernel(inner, x_ref, w_ref, cos_ref, sin_ref, q_ref, kv_ref):
    model = x_ref.shape[2]
    width = inner + 2 * KV_HEADS * HEAD_DIM
    tile = width // 128 * 128
    gain = column_row(w_ref[:, tile : tile + 128], width - tile, model)
    w_t = w_ref[...].T[:width, :]
    for s in range(2):
        x = x_ref[s].astype(f32)
        rho = lax.rsqrt(jnp.mean(x * x, axis=1, keepdims=True) + norm_eps)
        a = (x * rho * gain).astype(bf16)
        z = dot(w_t, a, NT)
        cos = cos_ref[s]
        sin = sin_ref[s]

        def rotated(head):
            u1 = z[head * HEAD_DIM : head * HEAD_DIM + HALF]
            u2 = z[head * HEAD_DIM + HALF : (head + 1) * HEAD_DIM]
            return jnp.concatenate([u1 * cos - u2 * sin, u2 * cos + u1 * sin], axis=0).astype(bf16)

        for head in range(HEADS):
            q_ref[s, head] = rotated(head) * jnp.asarray(0.125, bf16)
        for head in range(KV_HEADS):
            kv_ref[s, head] = rotated(HEADS + head)
            low = inner + (KV_HEADS + head) * HEAD_DIM
            kv_ref[s, KV_HEADS + head] = z[low : low + HEAD_DIM].astype(bf16)


def project(x, w, cos, sin):
    chunk = x.shape[1]
    return pl.pallas_call(
        functools.partial(qkv_kernel, HEADS * HEAD_DIM),
        out_shape=[
            jax.ShapeDtypeStruct((2, HEADS, HEAD_DIM, chunk), bf16),
            jax.ShapeDtypeStruct((2, 2 * KV_HEADS, HEAD_DIM, chunk), bf16),
        ],
        in_specs=[VMEM] * 4,
        out_specs=[VMEM] * 2,
        compiler_params=pltpu.CompilerParams(vmem_limit_bytes=56 << 20),
    )(x, w, cos, sin)


def order_kv(core, own_ref, other_ref, ordered):
    for core_is in range(2):

        @pl.when(core == core_is)
        def _():
            ordered[core_is] = own_ref[0]
            ordered[3 - core_is] = own_ref[1]
            ordered[1 - core_is] = other_ref[0]
            ordered[2 + core_is] = other_ref[1]


def visible(chunk, key_start, keys, lows, first_query, own, causal):
    size = lows.shape[1]
    shape = (keys, size - first_query)
    key = lax.broadcasted_iota(jnp.int32, shape, 0) + key_start
    seen = key >= lows[:, first_query:]
    if causal:
        query = lax.broadcasted_iota(jnp.int32, shape, 1) + (own + first_query)
        seen = seen & (key <= query)
    return seen


def forward_kernel(q_ref, own_ref, other_ref, low_ref, o_ref, lse_ref, kv, keys):
    core = lax.axis_index("dp") % 2
    chunk = q_ref.shape[3]
    half = chunk // 2
    order_kv(core, own_ref, other_ref, kv)
    for c in range(4):
        for g in range(KV_HEADS):
            keys[c, g] = kv[c, g].T

    def outer(step, carry):
        g = step // 2
        s = step % 2
        mine = jnp.where(s == 0, core, 3 - core)
        lows = low_ref[s]
        qs = [q_ref[s, GROUP * g + j] for j in range(GROUP)]

        def scores(c, k0, n, q0, causal):
            key_rows = keys[c, g, k0 : k0 + n, :]
            seen = visible(c, c * chunk + k0, n, lows, q0, mine * chunk, causal)
            raw = [dot(key_rows, q[:, q0:]) for q in qs]
            return [jnp.where(seen, r, NEG) for r in raw]

        def update(c, k0, n, masked, state):
            vals = kv[c, KV_HEADS + g, :, k0 : k0 + n]
            tops = [jnp.max(m, axis=0, keepdims=True) for m in masked]
            if state is not None:
                tops = [jnp.maximum(old[0], top) for old, top in zip(state, tops)]
            probs = [jnp.exp(m - top) for m, top in zip(masked, tops)]
            lows_ = [p.astype(bf16) for p in probs]
            sums = [jnp.sum(p, axis=0, keepdims=True) for p in probs]
            mixes = [dot(vals, p) for p in lows_]
            if state is None:
                return tuple(zip(tops, sums, mixes))
            new = []
            for old, top, total, mix in zip(state, tops, sums, mixes):
                shrink = jnp.exp(old[0] - top)
                new.append((top, old[1] * shrink + total, old[2] * shrink + mix))
            return tuple(new)

        early = scores(mine, 0, half, 0, True)
        late = scores(mine, half, half, half, True)
        first = update(mine, 0, half, early, None)
        second = update(
            mine, half, half, late, [tuple(part[:, half:] for part in item) for item in first]
        )
        state = tuple(
            tuple(jnp.concatenate([a[:, :half], b], axis=1) for a, b in zip(one, two))
            for one, two in zip(first, second)
        )
        state = lax.fori_loop(
            0,
            mine,
            lambda c, now: update(c, 0, chunk, scores(c, 0, chunk, 0, False), now),
            state,
        )
        for j in range(GROUP):
            top, total, mix = state[j]
            o_ref[s, GROUP * g + j] = (mix / total).astype(bf16)
            lse_ref[s, GROUP * g + j] = top + jnp.log(total)
        return carry

    lax.fori_loop(0, 2 * KV_HEADS, outer, 0)


def attend(q, own, other, lows):
    chunk = q.shape[3]
    return pl.pallas_call(
        forward_kernel,
        out_shape=[
            jax.ShapeDtypeStruct(q.shape, bf16),
            jax.ShapeDtypeStruct((2, HEADS, 1, chunk), f32),
        ],
        in_specs=[VMEM] * 4,
        out_specs=[VMEM] * 2,
        scratch_shapes=[
            pltpu.VMEM((4, 2 * KV_HEADS, HEAD_DIM, chunk), bf16),
            pltpu.VMEM((4, KV_HEADS, chunk, HEAD_DIM), bf16),
        ],
        compiler_params=pltpu.CompilerParams(vmem_limit_bytes=56 << 20),
    )(q, own, other, lows)


def backward_kernel(
    q_ref, own_ref, other_ref, low_ref, o_ref, lse_ref, do_ref, dq_ref, mine_ref, theirs_ref,
    kv, keys, values, dkv, dq_now,
):
    core = lax.axis_index("dp") % 2
    chunk = q_ref.shape[3]
    half = chunk // 2
    order_kv(core, own_ref, other_ref, kv)
    for c in range(4):
        for g in range(KV_HEADS):
            keys[c, g] = kv[c, g].T
            values[c, g] = kv[c, KV_HEADS + g].T
        for g in range(2 * KV_HEADS):
            dkv[c, g] = jnp.zeros((HEAD_DIM, chunk), f32)

    def outer(step, carry):
        g = step // 2
        s = step % 2
        mine = jnp.where(s == 0, core, 3 - core)
        lows = low_ref[s]
        qs = [q_ref[s, GROUP * g + j] for j in range(GROUP)]
        dos = [do_ref[s, GROUP * g + j] for j in range(GROUP)]
        lses = [lse_ref[s, GROUP * g + j] for j in range(GROUP)]
        deltas = [
            jnp.sum(
                dos[j].astype(f32) * o_ref[s, GROUP * g + j].astype(f32), axis=0, keepdims=True
            )
            for j in range(GROUP)
        ]

        def block(c, k0, n, q0, causal):
            key_rows = keys[c, g, k0 : k0 + n, :]
            value_rows = values[c, g, k0 : k0 + n, :]
            key_cols = kv[c, g, :, k0 : k0 + n]
            seen = visible(c, c * chunk + k0, n, lows, q0, mine * chunk, causal)
            raw = [dot(key_rows, q[:, q0:]) for q in qs]
            dps = [dot(value_rows, d[:, q0:]) for d in dos]
            probs = [
                jnp.exp(jnp.where(seen, r, NEG) - lse[:, q0:]) for r, lse in zip(raw, lses)
            ]
            lows_ = [p.astype(bf16) for p in probs]
            dss = [
                (p * (dp - delta[:, q0:])).astype(bf16)
                for p, dp, delta in zip(probs, dps, deltas)
            ]
            dkv[c, KV_HEADS + g, :, k0 : k0 + n] += dot(
                jnp.concatenate([d[:, q0:] for d in dos], axis=1),
                jnp.concatenate(lows_, axis=1),
                NT,
            )
            dkv[c, g, :, k0 : k0 + n] += dot(
                jnp.concatenate([q[:, q0:] for q in qs], axis=1),
                jnp.concatenate(dss, axis=1),
                NT,
            )
            return [dot(key_cols, ds) for ds in dss]

        early = block(mine, 0, half, 0, True)
        late = block(mine, half, half, half, True)
        for j in range(GROUP):
            dq_now[j] = jnp.concatenate(
                [early[j][:, :half], early[j][:, half:] + late[j]], axis=1
            )

        def inner(c, carry_in):
            more = block(c, 0, chunk, 0, False)
            for j in range(GROUP):
                dq_now[j] += more[j]
            return carry_in

        lax.fori_loop(0, mine, inner, 0)
        for j in range(GROUP):
            dq_ref[s, GROUP * g + j] = 0.125 * dq_now[j]
        return carry

    lax.fori_loop(0, 2 * KV_HEADS, outer, 0)
    for core_is in range(2):

        @pl.when(core == core_is)
        def _():
            mine_ref[0] = dkv[core_is]
            mine_ref[1] = dkv[3 - core_is]
            theirs_ref[0] = dkv[1 - core_is].astype(bf16)
            theirs_ref[1] = dkv[2 + core_is].astype(bf16)


def attend_back(q, own, other, lows, o, lse, do):
    chunk = q.shape[3]
    return pl.pallas_call(
        backward_kernel,
        out_shape=[
            jax.ShapeDtypeStruct(q.shape, f32),
            jax.ShapeDtypeStruct(own.shape, f32),
            jax.ShapeDtypeStruct(own.shape, bf16),
        ],
        in_specs=[VMEM] * 7,
        out_specs=[VMEM] * 3,
        scratch_shapes=[
            pltpu.VMEM((4, 2 * KV_HEADS, HEAD_DIM, chunk), bf16),
            pltpu.VMEM((4, KV_HEADS, chunk, HEAD_DIM), bf16),
            pltpu.VMEM((4, KV_HEADS, chunk, HEAD_DIM), bf16),
            pltpu.VMEM((4, 2 * KV_HEADS, HEAD_DIM, chunk), f32),
            pltpu.VMEM((GROUP, HEAD_DIM, chunk), f32),
        ],
        compiler_params=pltpu.CompilerParams(vmem_limit_bytes=58 << 20),
    )(q, own, other, lows, o, lse, do)


def feed_kernel(
    x_ref, o_ref, dy_ref, wide_ref, down_ref, out_ref, dm_ref, do_ref, gwide_ref, gdown_ref,
    act_s, dgu_s, a_s, dm_s, gain_s,
):
    rows_all, model = x_ref.shape
    hidden = down_ref.shape[0]
    inner = o_ref.shape[1]
    block = 256
    per = o_ref.shape[2] // block
    comb0 = 2 * hidden
    tile = (comb0 + model) // 128 * 128
    lane = comb0 + model - tile
    gain = column_row(wide_ref[:, tile : tile + 128], lane, model)
    gain_s[...] = jnp.zeros_like(gain_s)
    pieces = 3
    size = hidden // pieces

    def one(t, carry):
        rows = pl.ds(pl.multiple_of(t * block, block), block)
        cols = pl.ds(pl.multiple_of((t % per) * block, block), block)
        comb = wide_ref[:, comb0 : comb0 + model]
        m = x_ref[rows, :].astype(f32) + dot(o_ref[t // per, :, cols].T, comb)
        rho = lax.rsqrt(jnp.mean(m * m, axis=1, keepdims=True) + norm_eps)
        n = m * rho
        a = (n * gain).astype(bf16)
        a_s[rows, :] = a
        dy = dy_ref[rows, :]
        total = m
        da = None
        for f in range(pieces):
            low, high = f * size, (f + 1) * size
            w_g = wide_ref[:, low:high]
            w_u = wide_ref[:, hidden + low : hidden + high]
            w_d = down_ref[low:high, :]
            g = dot(a, w_g)
            u = dot(a, w_u)
            dact = dot(dy, w_d, NT)
            sig = 0.5 * jnp.tanh(0.5 * g) + 0.5
            silu = g * sig
            act = (silu * u).astype(bf16)
            du = (dact * silu).astype(bf16)
            dg = (dact * u * (sig + silu * (1.0 - sig))).astype(bf16)
            act_s[rows, low:high] = act
            dgu_s[rows, low:high] = dg
            dgu_s[rows, hidden + low : hidden + high] = du
            total = total + dot(act, w_d)
            part = dot(dg, w_g, NT) + dot(du, w_u, NT)
            da = part if da is None else da + part
        out_ref[rows, :] = total.astype(bf16)
        gain_s[...] += jnp.sum(da * n, axis=0, keepdims=True)
        dn = da * gain
        dm = dy.astype(f32) + rho * (dn - n * jnp.mean(dn * n, axis=1, keepdims=True))
        dm_ref[rows, :] = dm
        dm_low = dm.astype(bf16)
        dm_s[rows, :] = dm_low
        do_ref[t // per, :, cols] = dot(comb, dm_low, NT).astype(bf16)
        return carry

    lax.fori_loop(0, rows_all // block, one, 0)
    rows_d = 384

    def down_grad(i, carry):
        rows = pl.ds(pl.multiple_of(i * rows_d, 128), rows_d)
        gdown_ref[rows, :] = dot(act_s[:, rows].T, dy_ref[...]).astype(bf16)
        return carry

    lax.fori_loop(0, hidden // rows_d, down_grad, 0)
    a_t = a_s[...].T
    cols_w = 512

    def wide_grad(i, carry):
        cols = pl.ds(pl.multiple_of(i * cols_w, 128), cols_w)
        gwide_ref[:, cols] = dot(a_t, dgu_s[:, cols]).astype(bf16)
        return carry

    lax.fori_loop(0, 2 * hidden // cols_w, wide_grad, 0)
    chunk = o_ref.shape[2]
    comb_grad = dot(o_ref[0], dm_s[:chunk, :]) + dot(o_ref[1], dm_s[chunk:, :])
    gain_col = jnp.broadcast_to(gain_s[...], (128, model)).T
    end = gwide_ref.shape[1]
    gwide_ref[:, comb0:tile] = comb_grad[:, : tile - comb0].astype(bf16)
    gwide_ref[:, tile:end] = jnp.concatenate(
        [
            comb_grad[:, tile - comb0 :],
            gain_col[:, : 128 - lane],
            jnp.zeros((inner, end - tile - 128), f32),
        ],
        axis=1,
    ).astype(bf16)


def feed(x, o, dy, wide, down):
    rows, model = x.shape
    hidden = down.shape[0]
    return pl.pallas_call(
        feed_kernel,
        out_shape=[
            jax.ShapeDtypeStruct((rows, model), bf16),
            jax.ShapeDtypeStruct((rows, model), f32),
            jax.ShapeDtypeStruct(o.shape, bf16),
            jax.ShapeDtypeStruct(wide.shape, bf16),
            jax.ShapeDtypeStruct(down.shape, bf16),
        ],
        in_specs=[VMEM] * 5,
        out_specs=[VMEM] * 5,
        scratch_shapes=[
            pltpu.VMEM((rows, hidden), bf16),
            pltpu.VMEM((rows, 2 * hidden), bf16),
            pltpu.VMEM((rows, model), bf16),
            pltpu.VMEM((rows, model), bf16),
            pltpu.VMEM((1, model), f32),
        ],
        compiler_params=pltpu.CompilerParams(vmem_limit_bytes=60 << 20),
    )(x, o, dy, wide, down)


def qkv_back_kernel(
    inner, x_ref, dm_ref, dq_ref, own_ref, other_ref, cos_ref, sin_ref, w_ref, dx_ref, gw_ref
):
    model = x_ref.shape[2]
    width = inner + 2 * KV_HEADS * HEAD_DIM
    tile = width // 128 * 128
    lane = width - tile
    gain = column_row(w_ref[:, tile : tile + 128], lane, model)
    w = w_ref[:, :width]
    grad = None
    gain_grad = None
    for s in range(2):
        cos = cos_ref[s]
        sin = sin_ref[s]

        def back(d):
            d1 = d[:HALF]
            d2 = d[HALF:]
            return jnp.concatenate([d1 * cos + d2 * sin, d2 * cos - d1 * sin], axis=0)

        parts = [back(dq_ref[s, head]) for head in range(HEADS)]
        full = [own_ref[s, head] + other_ref[s, head].astype(f32) for head in range(2 * KV_HEADS)]
        parts += [back(full[head]) for head in range(KV_HEADS)]
        parts += full[KV_HEADS:]
        dz_t = jnp.concatenate([part.astype(bf16) for part in parts], axis=0)
        x = x_ref[s].astype(f32)
        rho = lax.rsqrt(jnp.mean(x * x, axis=1, keepdims=True) + norm_eps)
        n = x * rho
        a = (n * gain).astype(bf16)
        da = dot(dz_t.T, w, NT)
        part = dot(a.T, dz_t, NT)
        grad = part if grad is None else grad + part
        part = jnp.sum(da * n, axis=0, keepdims=True)
        gain_grad = part if gain_grad is None else gain_grad + part
        dn = da * gain
        dx = dm_ref[s] + rho * (dn - n * jnp.mean(dn * n, axis=1, keepdims=True))
        dx_ref[s] = dx.astype(bf16)
    gain_col = jnp.broadcast_to(gain_grad, (128, model)).T
    gw_ref[:, :tile] = grad[:, :tile].astype(bf16)
    gw_ref[:, tile:] = jnp.concatenate(
        [grad[:, tile:], gain_col[:, : gw_ref.shape[1] - width]], axis=1
    ).astype(bf16)


def project_back(x, dm, dq, own, other, cos, sin, w):
    return pl.pallas_call(
        functools.partial(qkv_back_kernel, HEADS * HEAD_DIM),
        out_shape=[jax.ShapeDtypeStruct(x.shape, bf16), jax.ShapeDtypeStruct(w.shape, bf16)],
        in_specs=[VMEM] * 8,
        out_specs=[VMEM] * 2,
        compiler_params=pltpu.CompilerParams(vmem_limit_bytes=58 << 20),
    )(x, dm, dq, own, other, cos, sin, w)


def routes(dp_size, seq_size):
    first, second = [], []
    taker = {0: 0, 3: 0, 1: 1, 2: 1}
    for dp in range(dp_size):
        core = dp % 2
        for j in range(4):
            k = 0 if j < 2 else 1
            source = dp * seq_size + j
            target = dp - core + taker[j]
            first.append((source, target * seq_size + 2 * core + k))
            second.append((source, target * seq_size + 2 * core + 1 - k))
    return first, second


def swap(pair, flip, perms):
    one = jnp.where(flip, pair[1], pair[0])
    two = jnp.where(flip, pair[0], pair[1])
    return (
        lax.ppermute(one, ("dp", "seq"), perms[0]),
        lax.ppermute(two, ("dp", "seq"), perms[1]),
    )


def unswap(one, two, flip):
    return jnp.stack([jnp.where(flip, two, one), jnp.where(flip, one, two)])


def adam_step(master, grad_total, mean_old, square_old, decays):
    mean_new = beta_one * mean_old + (1.0 - beta_one) * grad_total
    square_new = beta_two * square_old + (1.0 - beta_two) * grad_total * grad_total
    mean_hat = mean_new / (1.0 - beta_one**STEP)
    square_hat = square_new / (1.0 - beta_two**STEP)
    change = mean_hat / (jnp.sqrt(square_hat) + adam_eps)
    if decays:
        change = change + decay_rate * master
    return (master - learn_rate * change, mean_new, square_new)


def pad_cols(pieces, width):
    rows = pieces[0].shape[0]
    used = sum(piece.shape[1] for piece in pieces)
    return jnp.concatenate(
        [piece.astype(bf16) for piece in pieces] + [jnp.zeros((rows, width - used), bf16)], axis=1
    )


def on_device(
    tokens, positions, cotangent,
    balance, projector, combiner, leveler, expander, reducer,
    mean_balance, mean_projector, mean_combiner, mean_leveler, mean_expander, mean_reducer,
    square_balance, square_projector, square_combiner, square_leveler, square_expander,
    square_reducer,
):
    dp_size = lax.axis_size("dp")
    seq_size = lax.axis_size("seq")
    z = lax.axis_index("seq")
    core = lax.axis_index("dp") % 2
    _, chunk, model = tokens.shape
    width = projector.shape[1]
    hidden2 = expander.shape[1]
    inner = combiner.shape[1]
    perms = routes(dp_size, seq_size)
    backs = [[(b, a) for a, b in perm] for perm in perms]
    late = z >= 2
    odd = z % 2 == 1

    x1 = unswap(*swap(tokens, late, perms), odd)
    pos1 = unswap(*swap(positions, late, perms), odd)

    wide_part = pad_cols([expander, combiner, leveler[:, None]], 4096)
    proj_part = pad_cols([projector, balance[:, None]], 1024)
    wide, down, proj = gather_weights(
        [wide_part, reducer.astype(bf16), proj_part], [False, True, False], 0
    )

    inverse = jnp.power(rope_base, -jnp.arange(HALF, dtype=f32) * (2.0 / HEAD_DIM))
    phases = pos1.astype(f32)[:, None, :] * inverse[None, :, None]
    cos = jnp.cos(phases)
    sin = jnp.sin(phases)
    starts = jnp.stack([core * chunk, (3 - core) * chunk])
    index = starts[:, None] + jnp.arange(chunk, dtype=jnp.int32)[None, :]
    lows = (index - pos1)[:, None, :]

    q, own = project(x1, proj, cos, sin)
    dy_in, own = lax.optimization_barrier((cotangent, own))
    siblings = [
        (dp * seq_size + s, (dp + 1 - 2 * (dp % 2)) * seq_size + s)
        for dp in range(dp_size)
        for s in range(seq_size)
    ]
    other = lax.ppermute(own, ("dp", "seq"), siblings)
    dy1 = unswap(*swap(dy_in, late, perms), odd)
    o, lse = attend(q, own, other, lows)
    out1, dm, do, gwide, gdown = feed(
        x1.reshape(2 * chunk, model),
        o.reshape(2, inner, chunk),
        dy1.reshape(2 * chunk, model),
        wide,
        down,
    )
    out1 = out1.reshape(2, chunk, model)
    layer_out = unswap(*swap(out1, odd, backs), late)
    dq, own_grad, send_grad = attend_back(q, own, other, lows, o, lse, do.reshape(o.shape))
    other_grad = lax.ppermute(send_grad, ("dp", "seq"), siblings)
    dx1, gproj = project_back(
        x1, dm.reshape(2, chunk, model), dq, own_grad, other_grad, cos, sin, proj
    )
    tokens_grad = unswap(*swap(dx1, odd, backs), late)
    swide, sdown = scatter_grads([gwide, gdown], [False, True], 1)
    (sproj,) = scatter_grads([gproj], [False], 2)
    if dp_size > 8:
        groups = [[g * 8 + k for g in range(dp_size // 8)] for k in range(8)]
        swide, sdown, sproj = (
            lax.psum(part, "dp", axis_index_groups=groups) for part in (swide, sdown, sproj)
        )
    swide, sdown, sproj = (part.astype(f32) for part in (swide, sdown, sproj))
    totals = (
        sproj[:, width],
        sproj[:, :width],
        swide[:, hidden2 : hidden2 + inner],
        swide[:, hidden2 + inner],
        swide[:, :hidden2],
        sdown,
    )
    masters = (balance, projector, combiner, leveler, expander, reducer)
    means = (mean_balance, mean_projector, mean_combiner, mean_leveler, mean_expander, mean_reducer)
    squares = (
        square_balance, square_projector, square_combiner, square_leveler, square_expander,
        square_reducer,
    )
    decay_flags = (False, True, True, False, True, True)
    results = [
        adam_step(master, total, mean, square, decays)
        for master, total, mean, square, decays in zip(
            masters, totals, means, squares, decay_flags
        )
    ]
    return (
        (layer_out, tokens_grad)
        + totals
        + tuple(result[0] for result in results)
        + tuple(result[1] for result in results)
        + tuple(result[2] for result in results)
    )


def solution(mesh):
    vector, matrix = P("seq"), P("seq", None)
    weights = (vector, matrix, matrix, vector, matrix, matrix)
    rows = P("dp", "seq", None)
    return jax.shard_map(
        on_device,
        mesh=mesh,
        in_specs=(rows, P("dp", "seq"), rows) + weights * 3,
        out_specs=(rows, rows) + weights * 4,
        check_vma=False,
    )
```

```python
import functools

import jax
import jax.numpy as jnp
import numpy as np
from jax import lax
from jax.experimental import pallas as pl
from jax.experimental.pallas import tpu as pltpu
from jax.sharding import PartitionSpec as P

HEADS = 9
KV_HEADS = 3
HEAD_DIM = 64
HALF = HEAD_DIM // 2
GROUP = HEADS // KV_HEADS
STEP = 2

norm_eps = 1e-05
rope_base = 100000.0
beta_one = 0.9
beta_two = 0.95
adam_eps = 1e-08
learn_rate = 0.2
decay_rate = 0.1

bf16 = jnp.bfloat16
f32 = jnp.float32
NEG = -1e30
NN = (((1,), (0,)), ((), ()))
NT = (((1,), (1,)), ((), ()))
MESH = pl.DeviceIdType.MESH
VMEM = pl.BlockSpec(memory_space=pltpu.VMEM)
HBM = pl.BlockSpec(memory_space=pl.ANY)


def dot(left, right, dims=NN):
    return lax.dot_general(left, right, dims, preferred_element_type=f32)


class Place:
    def __init__(self):
        dp = lax.axis_index("dp")
        self.base = (dp // 8) * 8
        self.chip = (dp % 8) // 2
        self.core = dp % 2
        self.z = lax.axis_index("seq")

    def at(self, chip, core, z):
        return {"dp": self.base + 2 * chip + core, "seq": z}

    def sibling(self):
        return self.at(self.chip, 1 - self.core, self.z)

    def meet(self):
        barrier = pltpu.get_barrier_semaphore()
        for r in range(4):
            for c in range(2):
                if r + c > 0:
                    pl.semaphore_signal(
                        barrier,
                        inc=1,
                        device_id=self.at(self.chip, (self.core + c) % 2, (self.z + r) % 4),
                        device_id_type=MESH,
                    )
        for r in range(1, 4):
            pl.semaphore_signal(
                barrier,
                inc=1,
                device_id=self.at((self.chip + r) % 4, self.core, self.z),
                device_id_type=MESH,
            )
        return barrier

    def met(self, barrier):
        pl.semaphore_wait(barrier, 10)


def remote(src, dst, send_sem, recv_sem, target):
    return pltpu.make_async_remote_copy(
        src_ref=src,
        dst_ref=dst,
        send_sem=send_sem,
        recv_sem=recv_sem,
        device_id=target,
        device_id_type=MESH,
    )


class Exchange:
    def __init__(self, place, src, dst, sems, row, forward):
        self.place, self.src, self.dst, self.row = place, src, dst, row
        self.local, self.sent, self.got = sems
        z, core = place.z, place.core
        taker = ((z + 1) // 2) % 2
        if forward:
            self.goes = [(2 * core + i, taker) for i in range(2)]
            self.comes = [(core if i == 0 else 3 - core, z // 2) for i in range(2)]
            self.slot = z // 2
        else:
            self.goes = [(core if i == 0 else 3 - core, z // 2) for i in range(2)]
            self.comes = [(2 * core + i, taker) for i in range(2)]
            self.slot = z % 2

    def same(self, spot):
        return (spot[0] == self.place.z) & (spot[1] == self.place.core)

    def far(self, i):
        z, core = self.goes[i]
        return remote(
            self.src.at[i],
            self.dst.at[self.slot],
            self.sent.at[self.row, i],
            self.got.at[self.row, self.slot],
            self.place.at(self.place.chip, core, z),
        )

    def near(self, i):
        return pltpu.make_async_copy(
            self.src.at[i], self.dst.at[self.slot], self.local.at[self.row, i]
        )

    def start(self, i):
        @pl.when(self.same(self.goes[i]))
        def _():
            self.near(i).start()

        @pl.when(jnp.logical_not(self.same(self.goes[i])))
        def _():
            self.far(i).start()

    def arrive(self, i):
        @pl.when(jnp.logical_not(self.same(self.comes[i])))
        def _():
            remote(
                self.dst.at[i],
                self.dst.at[i],
                self.sent.at[self.row, i],
                self.got.at[self.row, i],
                self.place.sibling(),
            ).wait_recv()

    def near_done(self, i):
        @pl.when(self.same(self.goes[i]))
        def _():
            self.near(i).wait()

    def far_done(self, i):
        @pl.when(jnp.logical_not(self.same(self.goes[i])))
        def _():
            self.far(i).wait_send()


class Gather:
    def __init__(self, place, part, full, by_rows, sems, row):
        self.place, self.part, self.full, self.by_rows = place, part, full, by_rows
        self.local, self.sent, self.got = sems
        self.row = row
        self.rows = part.shape[0]
        self.size = (part.shape[0] if by_rows else part.shape[1]) // 8
        self.mine = 2 * place.chip + place.core

    def window(self, which, quarter):
        if self.by_rows:
            start = quarter * self.rows + which * self.size
            return (pl.ds(pl.multiple_of(start, 16), self.size), slice(None))
        return (
            pl.ds(pl.multiple_of(quarter * self.rows, 16), self.rows),
            pl.ds(pl.multiple_of(which * self.size, 128), self.size),
        )

    def copy(self, src, dst, slot, target):
        return remote(src, dst, self.sent.at[self.row, slot], self.got.at[self.row, slot], target)

    def own(self):
        start = pl.multiple_of(self.place.z * self.rows, 16)
        return pltpu.make_async_copy(
            self.part, self.full.at[pl.ds(start, self.rows), :], self.local.at[self.row]
        )

    def over_z(self, r):
        here = self.place
        return self.copy(
            self.part.at[self.window(self.mine, 0)],
            self.full.at[self.window(self.mine, here.z)],
            r - 1,
            here.at(here.chip, here.core, (here.z + r) % 4),
        )

    def spread(self, r):
        here = self.place
        ref = self.full.at[self.window(self.mine, (here.z + 4 - r) % 4)]
        copies = [
            self.copy(
                ref, ref, 3 * r + s - 1, here.at((here.chip + s) % 4, here.core, here.z)
            )
            for s in range(1, 4)
        ]
        return copies + [self.copy(ref, ref, 11 + r, here.sibling())]

    def hand_on(self, r, s):
        here = self.place
        which = 2 * ((here.chip + 4 - s) % 4) + here.core
        ref = self.full.at[self.window(which, (here.z + 4 - r) % 4)]
        return self.copy(ref, ref, 15 + 3 * (r - 1) + s - 1, here.sibling())

    def landed(self, which, r, slot):
        ref = self.full.at[self.window(which, (self.place.z + 4 - r) % 4)]
        self.copy(ref, ref, slot, self.place.sibling()).wait_recv()

    def first(self):
        self.own().start()
        for r in range(1, 4):
            self.over_z(r).start()

    def second(self):
        for r in range(1, 4):
            self.landed(self.mine, r, r - 1)
            for item in self.spread(r):
                item.start()

    def third(self):
        for r in range(1, 4):
            for s in range(1, 4):
                which = 2 * ((self.place.chip + 4 - s) % 4) + self.place.core
                self.landed(which, r, 3 * r + s - 1)
                self.hand_on(r, s).start()

    def finish(self):
        chip, other = self.place.chip, 1 - self.place.core
        for r in range(1, 4):
            self.landed(2 * chip + other, r, 11 + r)
            for s in range(1, 4):
                which = 2 * ((chip + 4 - s) % 4) + other
                self.landed(which, r, 15 + 3 * (r - 1) + s - 1)
        self.own().wait()

    def drain(self):
        for r in range(1, 4):
            self.over_z(r).wait_send()
            for item in self.spread(r):
                item.wait_send()
            for s in range(1, 4):
                self.hand_on(r, s).wait_send()


class Scatter:
    def __init__(self, place, grad, out, by_rows, scratch, sems, row):
        self.place, self.grad, self.out, self.by_rows = place, grad, out, by_rows
        self.mine_s, self.r0, self.r1, self.r2 = scratch
        self.local, self.sent, self.got = sems
        self.row = row
        self.size = (out.shape[0] if by_rows else out.shape[1]) // 8

    def block(self, which):
        if self.by_rows:
            return (pl.ds(pl.multiple_of(which * self.size, 16), self.size), slice(None))
        return (slice(None), pl.ds(pl.multiple_of(which * self.size, 128), self.size))

    def copy(self, src, dst, slot, target):
        return remote(src, dst, self.sent.at[self.row, slot], self.got.at[self.row, slot], target)

    def landed(self, ref, slot):
        self.copy(ref, ref, slot, self.place.sibling()).wait_recv()

    def own(self, s):
        here = self.place
        which = 2 * ((here.chip + s) % 4) + here.core
        return pltpu.make_async_copy(
            self.grad.at[(slice(None),) + self.block(which)],
            self.mine_s.at[s],
            self.local.at[self.row, s],
        )

    def to_sibling(self, s):
        here = self.place
        which = 2 * ((here.chip + s) % 4) + 1 - here.core
        return self.copy(
            self.grad.at[(slice(None),) + self.block(which)], self.r0.at[s], s, here.sibling()
        )

    def to_chip(self, s):
        here = self.place
        return self.copy(
            self.mine_s.at[s],
            self.r1.at[s - 1],
            3 + s,
            here.at((here.chip + s) % 4, here.core, here.z),
        )

    def to_z(self, r):
        here = self.place
        return self.copy(
            self.mine_s.at[0, (here.z + r) % 4],
            self.r2.at[r - 1],
            6 + r,
            here.at(here.chip, here.core, (here.z + r) % 4),
        )

    def spread(self):
        here = self.place
        ref = self.out.at[self.block(2 * here.chip + here.core)]
        copies = [
            self.copy(ref, ref, 9 + s, here.at((here.chip + s) % 4, here.core, here.z))
            for s in range(1, 4)
        ]
        return copies + [self.copy(ref, ref, 13, here.sibling())]

    def hand_on(self, s):
        here = self.place
        ref = self.out.at[self.block(2 * ((here.chip + 4 - s) % 4) + here.core)]
        return self.copy(ref, ref, 13 + s, here.sibling())

    def start(self):
        for s in (1, 2, 3, 0):
            self.to_sibling(s).start()
            self.own(s).start()

    def pair(self):
        for s in (1, 2, 3, 0):
            self.own(s).wait()
            self.landed(self.r0.at[s], s)
            total = self.mine_s[s].astype(f32) + self.r0[s].astype(f32)
            self.mine_s[s] = total.astype(bf16)
            if s > 0:
                self.to_chip(s).start()

    def plane(self):
        for s in range(1, 4):
            self.landed(self.r1.at[s - 1], 3 + s)
        total = self.mine_s[0].astype(f32)
        for s in range(1, 4):
            total = total + self.r1[s - 1].astype(f32)
        self.mine_s[0] = total.astype(bf16)
        for r in range(1, 4):
            self.to_z(r).start()

    def line(self):
        for r in range(1, 4):
            self.landed(self.r2.at[r - 1], 6 + r)
        total = self.mine_s[0, self.place.z].astype(f32)
        for r in range(1, 4):
            total = total + self.r2[r - 1].astype(f32)
        self.out[self.block(2 * self.place.chip + self.place.core)] = total.astype(bf16)
        for item in self.spread():
            item.start()

    def share(self):
        for s in range(1, 4):
            which = 2 * ((self.place.chip + 4 - s) % 4) + self.place.core
            self.landed(self.out.at[self.block(which)], 9 + s)
            self.hand_on(s).start()

    def finish(self):
        chip, other = self.place.chip, 1 - self.place.core
        self.landed(self.out.at[self.block(2 * chip + other)], 13)
        for s in range(1, 4):
            which = 2 * ((chip + 4 - s) % 4) + other
            self.landed(self.out.at[self.block(which)], 13 + s)

    def drain(self):
        for s in range(4):
            self.to_sibling(s).wait_send()
        for s in range(1, 4):
            self.to_chip(s).wait_send()
            self.to_z(s).wait_send()
            self.hand_on(s).wait_send()
        for item in self.spread():
            item.wait_send()


def scatter_part(array, by_rows):
    rows = array.shape[0] // 4
    return (4, rows // 8, array.shape[1]) if by_rows else (4, rows, array.shape[1] // 8)


def scatter_scratch(part):
    return [
        pltpu.VMEM((4,) + part, bf16),
        pltpu.VMEM((4,) + part, bf16),
        pltpu.VMEM((3,) + part, bf16),
        pltpu.VMEM((3,) + part[1:], bf16),
    ]


def column_row(tile, lane, height):
    return tile.astype(f32).T[lane : lane + 1, :]


def visible(key_start, keys, lows, first_query, own, causal):
    size = lows.shape[1]
    shape = (keys, size - first_query)
    key = lax.broadcasted_iota(jnp.int32, shape, 0) + key_start
    seen = key >= lows[:, first_query:]
    if causal:
        query = lax.broadcasted_iota(jnp.int32, shape, 1) + (own + first_query)
        seen = seen & (key <= query)
    return seen


def front_kernel(
    tokens, positions, cotangent, turns, balance, projector, combiner, leveler, expander,
    reducer, x_ref, dy_ref, q_ref, kv, o_ref, lse_ref, cos_ref, sin_ref, low_ref, proj, wide, down,
    keys, pos, proj_part, wide_part, down_part,
    ex_local, ex_sent, ex_got, ga_local, ga_sent, ga_got, kv_sent, kv_got,
):
    here = Place()
    core = here.core
    chunk = q_ref.shape[3]
    half = chunk // 2
    model = x_ref.shape[2]
    rows, width = projector.shape
    inner = combiner.shape[1]
    hidden2 = expander.shape[1]
    barrier = here.meet()

    def column(vector):
        return jnp.broadcast_to(vector[...], (128, rows)).T

    def pack(part, pieces, gain):
        at = 0
        for piece in pieces[:-1]:
            part[:, at : at + piece.shape[1]] = piece[...].astype(bf16)
            at += piece.shape[1]
        last = pieces[-1]
        cut = last.shape[1] // 128 * 128
        part[:, at : at + cut] = last[:, :cut].astype(bf16)
        rest = last.shape[1] - cut
        end = part.shape[1] - at - cut - 128
        tail = [last[:, cut:], column(gain)[:, : 128 - rest]]
        if end > 0:
            tail.append(jnp.zeros((rows, end), f32))
        part[:, at + cut :] = jnp.concatenate(tail, axis=1).astype(bf16)

    pack(proj_part, [projector], balance)
    here.met(barrier)
    ga = (ga_local, ga_sent, ga_got)
    ex = (ex_local, ex_sent, ex_got)
    proj_in = Gather(here, proj_part, proj, False, ga, 0)
    wide_in = Gather(here, wide_part, wide, False, ga, 1)
    down_in = Gather(here, down_part, down, True, ga, 2)
    pos_in = Exchange(here, positions, pos, ex, 0, True)
    x_in = Exchange(here, tokens, x_ref, ex, 1, True)
    dy_in = Exchange(here, cotangent, dy_ref, ex, 2, True)
    proj_in.first()
    for i in range(2):
        pos_in.start(i)
    for i in range(2):
        x_in.start(i)
    pack(wide_part, [expander, combiner], leveler)
    down_part[...] = reducer[...].astype(bf16)

    for i in range(2):
        pos_in.near_done(i)
    for i in range(2):
        pos_in.arrive(i)
    inverse = jnp.concatenate([turns[...]] * (chunk // 128), axis=1)
    for s in range(2):
        row = jnp.concatenate([pos[s, i : i + 1, :] for i in range(chunk // 128)], axis=1)
        phases = row.astype(f32) * inverse
        cos_ref[s] = jnp.cos(phases)
        sin_ref[s] = jnp.sin(phases)
        start = (core if s == 0 else 3 - core) * chunk
        low_ref[s] = lax.broadcasted_iota(jnp.int32, (1, chunk), 1) + start - row

    proj_in.second()
    proj_in.third()
    proj_in.finish()
    tile = width // 128 * 128
    gain = column_row(proj[:, tile : tile + 128], width - tile, model)
    w_t = proj[...].T[:width, :]

    def kv_copy(s):
        mine = core if s == 0 else 3 - core
        return remote(
            kv.at[mine], kv.at[mine], kv_sent.at[s], kv_got.at[s], here.sibling()
        )

    for i in range(2):
        x_in.near_done(i)
    for s in range(2):
        x_in.arrive(s)
        if s == 1:
            wide_in.first()
            down_in.first()
            for i in range(2):
                dy_in.start(i)
        x = x_ref[s].astype(f32)
        rho = lax.rsqrt(jnp.mean(x * x, axis=1, keepdims=True) + norm_eps)
        a = (x * rho * gain).astype(bf16)
        zs = dot(w_t, a, NT)
        cos = cos_ref[s]
        sin = sin_ref[s]
        mine = core if s == 0 else 3 - core

        def rotated(head):
            u1 = zs[head * HEAD_DIM : head * HEAD_DIM + HALF]
            u2 = zs[head * HEAD_DIM + HALF : (head + 1) * HEAD_DIM]
            return jnp.concatenate([u1 * cos - u2 * sin, u2 * cos + u1 * sin], axis=0).astype(bf16)

        for head in range(KV_HEADS):
            kv[mine, head] = rotated(HEADS + head)
            low = inner + (KV_HEADS + head) * HEAD_DIM
            kv[mine, KV_HEADS + head] = zs[low : low + HEAD_DIM].astype(bf16)
        kv_copy(s).start()
        for head in range(HEADS):
            q_ref[s, head] = rotated(head) * jnp.asarray(0.125, bf16)
    for s in range(2):
        theirs = 1 - core if s == 0 else 2 + core
        remote(
            kv.at[theirs], kv.at[theirs], kv_sent.at[s], kv_got.at[s], here.sibling()
        ).wait_recv()
    for s in range(2):
        kv_copy(s).wait_send()

    for c in range(4):
        for g in range(KV_HEADS):
            keys[c, g] = kv[c, g].T

    def outer(step, carry):
        g = step // 2
        s = step % 2
        mine = core + s * (3 - 2 * core)
        lows = low_ref[s]
        qs = [q_ref[s, GROUP * g + j] for j in range(GROUP)]

        @pl.when(step == 2)
        def _():
            wide_in.second()
            down_in.second()

        def scores(c, k0, n, q0, causal):
            key_rows = keys[c, g, k0 : k0 + n, :]
            seen = visible(c * chunk + k0, n, lows, q0, mine * chunk, causal)
            raw = [dot(key_rows, q[:, q0:]) for q in qs]
            return [jnp.where(seen, r, NEG) for r in raw]

        def update(c, k0, n, masked, state):
            vals = kv[c, KV_HEADS + g, :, k0 : k0 + n]
            tops = [jnp.max(m, axis=0, keepdims=True) for m in masked]
            if state is not None:
                tops = [jnp.maximum(old[0], top) for old, top in zip(state, tops)]
            probs = [jnp.exp(m - top) for m, top in zip(masked, tops)]
            lows_ = [p.astype(bf16) for p in probs]
            sums = [jnp.sum(p, axis=0, keepdims=True) for p in probs]
            mixes = [dot(vals, p) for p in lows_]
            if state is None:
                return tuple(zip(tops, sums, mixes))
            new = []
            for old, top, total, mix in zip(state, tops, sums, mixes):
                shrink = jnp.exp(old[0] - top)
                new.append((top, old[1] * shrink + total, old[2] * shrink + mix))
            return tuple(new)

        early = scores(mine, 0, half, 0, True)
        late = scores(mine, half, half, half, True)
        first = update(mine, 0, half, early, None)
        second = update(
            mine, half, half, late, [tuple(part[:, half:] for part in item) for item in first]
        )
        state = tuple(
            tuple(jnp.concatenate([a[:, :half], b], axis=1) for a, b in zip(one, two))
            for one, two in zip(first, second)
        )
        state = lax.fori_loop(
            0,
            mine,
            lambda c, now: update(c, 0, chunk, scores(c, 0, chunk, 0, False), now),
            state,
        )
        for j in range(GROUP):
            top, total, mix = state[j]
            o_ref[s, GROUP * g + j] = (mix / total).astype(bf16)
            lse_ref[s, GROUP * g + j] = top + jnp.log(total)
        return carry

    lax.fori_loop(0, 2 * KV_HEADS, outer, 0)
    for item in (wide_in, down_in):
        item.third()
    for i in range(2):
        dy_in.near_done(i)
        dy_in.arrive(i)
    for item in (wide_in, down_in):
        item.finish()
    for item in (proj_in, wide_in, down_in):
        item.drain()
    for item in (pos_in, x_in, dy_in):
        for i in range(2):
            item.far_done(i)


def front(tokens, positions, cotangent, weights):
    _, chunk, model = tokens.shape
    rows, width = weights[1].shape
    hidden = weights[5].shape[0]
    sd = jax.ShapeDtypeStruct
    exponent = np.arange(HALF, dtype=np.float32) * np.float32(2.0 / HEAD_DIM)
    turns = np.power(np.float32(rope_base), -exponent).astype(np.float32)
    turns = jnp.asarray(np.broadcast_to(turns[:, None], (HALF, 128)))
    outs = [
        (sd(tokens.shape, bf16), VMEM),
        (sd(tokens.shape, bf16), HBM),
        (sd((2, HEADS, HEAD_DIM, chunk), bf16), VMEM),
        (sd((4, 2 * KV_HEADS, HEAD_DIM, chunk), bf16), VMEM),
        (sd((2, HEADS, HEAD_DIM, chunk), bf16), VMEM),
        (sd((2, HEADS, 1, chunk), f32), VMEM),
        (sd((2, HALF, chunk), f32), VMEM),
        (sd((2, HALF, chunk), f32), VMEM),
        (sd((2, 1, chunk), jnp.int32), VMEM),
        (sd((4 * rows, 1024), bf16), VMEM),
        (sd((4 * rows, 4096), bf16), HBM),
        (sd((4 * hidden, model), bf16), HBM),
    ]
    return pl.pallas_call(
        front_kernel,
        out_shape=[shape for shape, _ in outs],
        in_specs=[HBM, VMEM, HBM] + [VMEM] * 7,
        out_specs=[spec for _, spec in outs],
        scratch_shapes=[
            pltpu.VMEM((4, KV_HEADS, chunk, HEAD_DIM), bf16),
            pltpu.VMEM((2, chunk // 128, 128), jnp.int32),
            pltpu.VMEM((rows, 1024), bf16),
            pltpu.VMEM((rows, 4096), bf16),
            pltpu.VMEM((hidden, model), bf16),
            pltpu.SemaphoreType.DMA((3, 2)),
            pltpu.SemaphoreType.DMA((3, 2)),
            pltpu.SemaphoreType.DMA((3, 2)),
            pltpu.SemaphoreType.DMA((3,)),
            pltpu.SemaphoreType.DMA((3, 24)),
            pltpu.SemaphoreType.DMA((3, 24)),
            pltpu.SemaphoreType.DMA((2,)),
            pltpu.SemaphoreType.DMA((2,)),
        ],
        compiler_params=pltpu.CompilerParams(
            collective_id=0, has_side_effects=True, vmem_limit_bytes=58 << 20
        ),
    )(tokens, positions.reshape(2, chunk // 128, 128), cotangent, turns, *weights)


def feed_kernel(
    x_ref, o_ref, dy_ref, wide_ref, down_ref, out_ref, dm_ref, do_ref, gwide_ref, gdown_ref,
    act_s, dgu_s, a_s, dm_s, gain_s,
):
    rows_all, model = x_ref.shape
    hidden = down_ref.shape[0]
    inner = o_ref.shape[1]
    block = 256
    per = o_ref.shape[2] // block
    comb0 = 2 * hidden
    tile = (comb0 + model) // 128 * 128
    lane = comb0 + model - tile
    gain = column_row(wide_ref[:, tile : tile + 128], lane, model)
    gain_s[...] = jnp.zeros_like(gain_s)
    pieces = 3
    size = hidden // pieces

    def one(t, carry):
        rows = pl.ds(pl.multiple_of(t * block, block), block)
        cols = pl.ds(pl.multiple_of((t % per) * block, block), block)
        comb = wide_ref[:, comb0 : comb0 + model]
        m = x_ref[rows, :].astype(f32) + dot(o_ref[t // per, :, cols].T, comb)
        rho = lax.rsqrt(jnp.mean(m * m, axis=1, keepdims=True) + norm_eps)
        n = m * rho
        a = (n * gain).astype(bf16)
        a_s[rows, :] = a
        dy = dy_ref[rows, :]
        total = m
        da = None
        for f in range(pieces):
            low, high = f * size, (f + 1) * size
            w_g = wide_ref[:, low:high]
            w_u = wide_ref[:, hidden + low : hidden + high]
            w_d = down_ref[low:high, :]
            g = dot(a, w_g)
            u = dot(a, w_u)
            dact = dot(dy, w_d, NT)
            sig = 0.5 * jnp.tanh(0.5 * g) + 0.5
            silu = g * sig
            act = (silu * u).astype(bf16)
            du = (dact * silu).astype(bf16)
            dg = (dact * u * (sig + silu * (1.0 - sig))).astype(bf16)
            act_s[rows, low:high] = act
            dgu_s[rows, low:high] = dg
            dgu_s[rows, hidden + low : hidden + high] = du
            total = total + dot(act, w_d)
            part = dot(dg, w_g, NT) + dot(du, w_u, NT)
            da = part if da is None else da + part
        out_ref[rows, :] = total.astype(bf16)
        gain_s[...] += jnp.sum(da * n, axis=0, keepdims=True)
        dn = da * gain
        dm = dy.astype(f32) + rho * (dn - n * jnp.mean(dn * n, axis=1, keepdims=True))
        dm_ref[rows, :] = dm
        dm_low = dm.astype(bf16)
        dm_s[rows, :] = dm_low
        do_ref[t // per, :, cols] = dot(comb, dm_low, NT).astype(bf16)
        return carry

    lax.fori_loop(0, rows_all // block, one, 0)
    rows_d = 384

    def down_grad(i, carry):
        rows = pl.ds(pl.multiple_of(i * rows_d, 128), rows_d)
        gdown_ref[rows, :] = dot(act_s[:, rows].T, dy_ref[...]).astype(bf16)
        return carry

    lax.fori_loop(0, hidden // rows_d, down_grad, 0)
    a_t = a_s[...].T
    cols_w = 512

    def wide_grad(i, carry):
        cols = pl.ds(pl.multiple_of(i * cols_w, 128), cols_w)
        gwide_ref[:, cols] = dot(a_t, dgu_s[:, cols]).astype(bf16)
        return carry

    lax.fori_loop(0, 2 * hidden // cols_w, wide_grad, 0)
    chunk = o_ref.shape[2]
    comb_grad = dot(o_ref[0], dm_s[:chunk, :]) + dot(o_ref[1], dm_s[chunk:, :])
    gain_col = jnp.broadcast_to(gain_s[...], (128, model)).T
    end = gwide_ref.shape[1]
    gwide_ref[:, comb0:tile] = comb_grad[:, : tile - comb0].astype(bf16)
    gwide_ref[:, tile:end] = jnp.concatenate(
        [
            comb_grad[:, tile - comb0 :],
            gain_col[:, : 128 - lane],
            jnp.zeros((inner, end - tile - 128), f32),
        ],
        axis=1,
    ).astype(bf16)


def feed(x, o, dy, wide, down):
    rows, model = x.shape
    hidden = down.shape[0]
    return pl.pallas_call(
        feed_kernel,
        out_shape=[
            jax.ShapeDtypeStruct((rows, model), bf16),
            jax.ShapeDtypeStruct((rows, model), f32),
            jax.ShapeDtypeStruct(o.shape, bf16),
            jax.ShapeDtypeStruct(wide.shape, bf16),
            jax.ShapeDtypeStruct(down.shape, bf16),
        ],
        in_specs=[VMEM] * 5,
        out_specs=[VMEM] * 5,
        scratch_shapes=[
            pltpu.VMEM((rows, hidden), bf16),
            pltpu.VMEM((rows, 2 * hidden), bf16),
            pltpu.VMEM((rows, model), bf16),
            pltpu.VMEM((rows, model), bf16),
            pltpu.VMEM((1, model), f32),
        ],
        compiler_params=pltpu.CompilerParams(vmem_limit_bytes=60 << 20),
    )(x, o, dy, wide, down)


def back_kernel(
    inner,
    q_ref, kv, o_ref, lse_ref, do_ref, cos_ref, sin_ref, low_ref, x_any, dm_any, proj_any,
    gwide, gdown, out_any,
    layer_ref, dx_ref, swide, sdown, sproj,
    keys, values, dkv, dq, dq_now, give, take, x_ref, dm_ref, proj, dx_s, gproj,
    wide_a, wide_b, wide_c, wide_d, down_a, down_b, down_c, down_d,
    proj_a, proj_b, proj_c, proj_d,
    load, ex_local, ex_sent, ex_got, sc_local, sc_sent, sc_got, kv_sent, kv_got,
):
    here = Place()
    core = here.core
    chunk = q_ref.shape[3]
    half = chunk // 2
    model = x_ref.shape[2]
    width = inner + 2 * KV_HEADS * HEAD_DIM
    barrier = here.meet()
    loads = [
        pltpu.make_async_copy(src, dst, load.at[i])
        for i, (src, dst) in enumerate(((x_any, x_ref), (dm_any, dm_ref), (proj_any, proj)))
    ]
    for item in loads:
        item.start()
    here.met(barrier)
    sc = (sc_local, sc_sent, sc_got)
    ex = (ex_local, ex_sent, ex_got)
    down_sum = Scatter(here, gdown, sdown, True, (down_a, down_b, down_c, down_d), sc, 0)
    wide_sum = Scatter(here, gwide, swide, False, (wide_a, wide_b, wide_c, wide_d), sc, 1)
    proj_sum = Scatter(here, gproj, sproj, False, (proj_a, proj_b, proj_c, proj_d), sc, 2)
    out_back = Exchange(here, out_any, layer_ref, ex, 0, False)
    dx_back = Exchange(here, dx_s, dx_ref, ex, 1, False)
    down_sum.start()
    wide_sum.start()
    for i in range(2):
        out_back.start(i)

    for c in range(4):
        for g in range(KV_HEADS):
            keys[c, g] = kv[c, g].T
            values[c, g] = kv[c, KV_HEADS + g].T
        for g in range(2 * KV_HEADS):
            dkv[c, g] = jnp.zeros((HEAD_DIM, chunk), f32)

    def outer(step, carry):
        g = step // 2
        s = step % 2
        mine = core + s * (3 - 2 * core)
        lows = low_ref[s]

        @pl.when(step == 1)
        def _():
            down_sum.pair()

        @pl.when(step == 2)
        def _():
            wide_sum.pair()

        @pl.when(step == 4)
        def _():
            down_sum.plane()

        @pl.when(step == 5)
        def _():
            down_sum.line()

        qs = [q_ref[s, GROUP * g + j] for j in range(GROUP)]
        dos = [do_ref[s, GROUP * g + j] for j in range(GROUP)]
        lses = [lse_ref[s, GROUP * g + j] for j in range(GROUP)]
        deltas = [
            jnp.sum(
                dos[j].astype(f32) * o_ref[s, GROUP * g + j].astype(f32), axis=0, keepdims=True
            )
            for j in range(GROUP)
        ]

        def block(c, k0, n, q0, causal):
            key_rows = keys[c, g, k0 : k0 + n, :]
            value_rows = values[c, g, k0 : k0 + n, :]
            key_cols = kv[c, g, :, k0 : k0 + n]
            seen = visible(c * chunk + k0, n, lows, q0, mine * chunk, causal)
            raw = [dot(key_rows, q[:, q0:]) for q in qs]
            dps = [dot(value_rows, d[:, q0:]) for d in dos]
            probs = [
                jnp.exp(jnp.where(seen, r, NEG) - lse[:, q0:]) for r, lse in zip(raw, lses)
            ]
            lows_ = [p.astype(bf16) for p in probs]
            dss = [
                (p * (dp - delta[:, q0:])).astype(bf16)
                for p, dp, delta in zip(probs, dps, deltas)
            ]
            dkv[c, KV_HEADS + g, :, k0 : k0 + n] += dot(
                jnp.concatenate([d[:, q0:] for d in dos], axis=1),
                jnp.concatenate(lows_, axis=1),
                NT,
            )
            dkv[c, g, :, k0 : k0 + n] += dot(
                jnp.concatenate([q[:, q0:] for q in qs], axis=1),
                jnp.concatenate(dss, axis=1),
                NT,
            )
            return [dot(key_cols, ds) for ds in dss]

        early = block(mine, 0, half, 0, True)
        late = block(mine, half, half, half, True)
        for j in range(GROUP):
            dq_now[j] = jnp.concatenate(
                [early[j][:, :half], early[j][:, half:] + late[j]], axis=1
            )

        def more(c, carry_in):
            extra = block(c, 0, chunk, 0, False)
            for j in range(GROUP):
                dq_now[j] += extra[j]
            return carry_in

        lax.fori_loop(0, mine, more, 0)
        for j in range(GROUP):
            dq[s, GROUP * g + j] = 0.125 * dq_now[j]
        return carry

    lax.fori_loop(0, 2 * KV_HEADS, outer, 0)

    def give_copy(s):
        return remote(give.at[s], take.at[s], kv_sent.at[s], kv_got.at[s], here.sibling())

    for s in range(2):
        theirs = 1 - core if s == 0 else 2 + core
        give[s] = dkv[theirs].astype(bf16)
        give_copy(s).start()
    for item in loads:
        item.wait()
    tile = width // 128 * 128
    lane = width - tile
    gain = column_row(proj[:, tile : tile + 128], lane, model)
    w = proj[:, :width]
    grad = None
    gain_grad = None
    for s in range(2):
        cos = cos_ref[s]
        sin = sin_ref[s]
        mine = core if s == 0 else 3 - core

        def turned(d):
            d1 = d[:HALF]
            d2 = d[HALF:]
            return jnp.concatenate([d1 * cos + d2 * sin, d2 * cos - d1 * sin], axis=0)

        give_copy(s).wait_recv()
        parts = [turned(dq[s, head]) for head in range(HEADS)]
        full = [dkv[mine, head] + take[s, head].astype(f32) for head in range(2 * KV_HEADS)]
        parts += [turned(full[head]) for head in range(KV_HEADS)]
        parts += full[KV_HEADS:]
        dz_t = jnp.concatenate([part.astype(bf16) for part in parts], axis=0)
        x = x_ref[s].astype(f32)
        rho = lax.rsqrt(jnp.mean(x * x, axis=1, keepdims=True) + norm_eps)
        n = x * rho
        a = (n * gain).astype(bf16)
        da = dot(dz_t.T, w, NT)
        dn = da * gain
        dx = dm_ref[s] + rho * (dn - n * jnp.mean(dn * n, axis=1, keepdims=True))
        dx_s[s] = dx.astype(bf16)
        dx_back.start(s)
        part = dot(a.T, dz_t, NT)
        grad = part if grad is None else grad + part
        part = jnp.sum(da * n, axis=0, keepdims=True)
        gain_grad = part if gain_grad is None else gain_grad + part
    gain_col = jnp.broadcast_to(gain_grad, (128, model)).T
    full = jnp.concatenate([grad, gain_col[:, : sproj.shape[1] - width]], axis=1).astype(bf16)
    rows = model // 4
    for quarter in range(4):
        gproj[quarter] = full[quarter * rows : (quarter + 1) * rows, :]
    proj_sum.start()
    wide_sum.plane()
    proj_sum.pair()
    down_sum.share()
    wide_sum.line()
    proj_sum.plane()
    wide_sum.share()
    proj_sum.line()
    proj_sum.share()
    for item in (down_sum, wide_sum, proj_sum):
        item.finish()
        item.drain()
    for item in (out_back, dx_back):
        for i in range(2):
            item.near_done(i)
            item.arrive(i)
            item.far_done(i)
    for s in range(2):
        give_copy(s).wait_send()


def back(q, kv, o, lse, do, cos, sin, lows, x, dm, proj, gwide, gdown, out):
    chunk = q.shape[3]
    model = x.shape[2]
    inner = HEADS * HEAD_DIM
    sd = jax.ShapeDtypeStruct
    wide_rows, down_rows = gwide.shape[0] // 4, gdown.shape[0] // 4
    scratch = [
        pltpu.VMEM((4, KV_HEADS, chunk, HEAD_DIM), bf16),
        pltpu.VMEM((4, KV_HEADS, chunk, HEAD_DIM), bf16),
        pltpu.VMEM((4, 2 * KV_HEADS, HEAD_DIM, chunk), f32),
        pltpu.VMEM((2, HEADS, HEAD_DIM, chunk), f32),
        pltpu.VMEM((GROUP, HEAD_DIM, chunk), f32),
        pltpu.VMEM((2, 2 * KV_HEADS, HEAD_DIM, chunk), bf16),
        pltpu.VMEM((2, 2 * KV_HEADS, HEAD_DIM, chunk), bf16),
        pltpu.VMEM(x.shape, bf16),
        pltpu.VMEM(x.shape, f32),
        pltpu.VMEM(proj.shape, bf16),
        pltpu.VMEM(x.shape, bf16),
        pltpu.VMEM((4, proj.shape[0] // 4, proj.shape[1]), bf16),
    ]
    for array, by_rows in ((gwide, False), (gdown, True), (proj, False)):
        scratch += scatter_scratch(scatter_part(array, by_rows))
    scratch += [
        pltpu.SemaphoreType.DMA((3,)),
        pltpu.SemaphoreType.DMA((2, 2)),
        pltpu.SemaphoreType.DMA((2, 2)),
        pltpu.SemaphoreType.DMA((2, 2)),
        pltpu.SemaphoreType.DMA((3, 4)),
        pltpu.SemaphoreType.DMA((3, 17)),
        pltpu.SemaphoreType.DMA((3, 17)),
        pltpu.SemaphoreType.DMA((2,)),
        pltpu.SemaphoreType.DMA((2,)),
    ]
    return pl.pallas_call(
        functools.partial(back_kernel, inner),
        out_shape=[
            sd(x.shape, bf16),
            sd(x.shape, bf16),
            sd((wide_rows, gwide.shape[1]), bf16),
            sd((down_rows, gdown.shape[1]), bf16),
            sd((proj.shape[0] // 4, proj.shape[1]), bf16),
        ],
        in_specs=[VMEM] * 8 + [HBM] * 6,
        out_specs=[HBM, HBM, VMEM, VMEM, VMEM],
        scratch_shapes=scratch,
        compiler_params=pltpu.CompilerParams(
            collective_id=1, has_side_effects=True, vmem_limit_bytes=60 << 20
        ),
    )(
        q, kv, o, lse, do, cos, sin, lows, x, dm, proj,
        gwide.reshape(4, wide_rows, gwide.shape[1]),
        gdown.reshape(4, down_rows, gdown.shape[1]),
        out,
    )


def adam_values(master, grad, mean, square, decays):
    mean_new = beta_one * mean + (1.0 - beta_one) * grad
    square_new = beta_two * square + (1.0 - beta_two) * grad * grad
    mean_hat = mean_new / (1.0 - beta_one**STEP)
    square_hat = square_new / (1.0 - beta_two**STEP)
    change = mean_hat / (jnp.sqrt(square_hat) + adam_eps)
    if decays:
        change = change + decay_rate * master
    return master - learn_rate * change, mean_new, square_new


def adam_kernel(decay_flags, swide, sdown, sproj, *refs):
    masters, means, squares = refs[:6], refs[6:12], refs[12:18]
    totals, nexts, new_means, new_squares = (refs[18 + 6 * k : 24 + 6 * k] for k in range(4))
    width = masters[1].shape[1]
    inner = masters[2].shape[1]
    hidden2 = masters[4].shape[1]

    def row_of(ref, column):
        tile = column // 128 * 128
        return column_row(ref[:, tile : tile + 128], column - tile, ref.shape[0])

    grads = (
        lambda: row_of(sproj, width),
        lambda: sproj[:, :width].astype(f32),
        lambda: swide[:, hidden2 : hidden2 + inner].astype(f32),
        lambda: row_of(swide, hidden2 + inner),
        lambda: swide[:, :hidden2].astype(f32),
        lambda: sdown[...].astype(f32),
    )
    for i in range(6):
        grad = grads[i]()
        totals[i][...] = grad
        nexts[i][...], new_means[i][...], new_squares[i][...] = adam_values(
            masters[i][...], grad, means[i][...], squares[i][...], decay_flags[i]
        )


def optimize(sums, masters, means, squares):
    decay_flags = (False, True, True, False, True, True)
    arrays = [a[None, :] if a.ndim == 1 else a for a in masters + means + squares]
    shapes = [jax.ShapeDtypeStruct(a.shape, f32) for a in arrays[:6]] * 4
    results = pl.pallas_call(
        functools.partial(adam_kernel, decay_flags),
        out_shape=shapes,
        in_specs=[VMEM] * 21,
        out_specs=[VMEM] * 24,
        compiler_params=pltpu.CompilerParams(vmem_limit_bytes=60 << 20),
    )(*sums, *arrays)
    return tuple(r.reshape(m.shape) for r, m in zip(results, masters * 4))


def on_device(tokens, positions, cotangent, *rest):
    masters, means, squares = rest[:6], rest[6:12], rest[12:18]
    dp_size = lax.axis_size("dp")
    _, chunk, model = tokens.shape
    inner = HEADS * HEAD_DIM
    weights = [a[None, :] if a.ndim == 1 else a for a in masters]
    x, dy, q, kv, o, lse, cos, sin, lows, proj, wide, down = front(
        tokens, positions, cotangent, weights
    )
    out, dm, do, gwide, gdown = feed(
        x.reshape(2 * chunk, model),
        o.reshape(2, inner, chunk),
        dy.reshape(2 * chunk, model),
        wide,
        down,
    )
    layer_out, tokens_grad, *sums = back(
        q, kv, o, lse, do.reshape(o.shape), cos, sin, lows, x, dm.reshape(x.shape), proj,
        gwide, gdown, out.reshape(x.shape),
    )
    if dp_size > 8:
        groups = [[g * 8 + k for g in range(dp_size // 8)] for k in range(8)]
        sums = [lax.psum(part, "dp", axis_index_groups=groups) for part in sums]
    return (layer_out, tokens_grad) + optimize(sums, masters, means, squares)


def solution(mesh):
    vector, matrix = P("seq"), P("seq", None)
    weights = (vector, matrix, matrix, vector, matrix, matrix)
    rows = P("dp", "seq", None)
    return jax.shard_map(
        on_device,
        mesh=mesh,
        in_specs=(rows, P("dp", "seq"), rows) + weights * 3,
        out_specs=(rows, rows) + weights * 4,
        check_vma=False,
    )
```

```python
import functools

import jax
import jax.numpy as jnp
import numpy as np
from jax import lax
from jax.experimental import pallas as pl
from jax.experimental.pallas import tpu as pltpu
from jax.sharding import PartitionSpec as P

HEADS = 9
KV_HEADS = 3
HEAD_DIM = 64
HALF = HEAD_DIM // 2
GROUP = HEADS // KV_HEADS
STEP = 2

norm_eps = 1e-05
rope_base = 100000.0
beta_one = 0.9
beta_two = 0.95
adam_eps = 1e-08
learn_rate = 0.2
decay_rate = 0.1

bf16 = jnp.bfloat16
f32 = jnp.float32
NEG = -1e30
NN = (((1,), (0,)), ((), ()))
NT = (((1,), (1,)), ((), ()))
MESH = pl.DeviceIdType.MESH
VMEM = pl.BlockSpec(memory_space=pltpu.VMEM)
HBM = pl.BlockSpec(memory_space=pl.ANY)


def dot(left, right, dims=NN):
    return lax.dot_general(left, right, dims, preferred_element_type=f32)


class Place:
    def __init__(self):
        dp = lax.axis_index("dp")
        self.base = (dp // 8) * 8
        self.chip = (dp % 8) // 2
        self.core = dp % 2
        self.z = lax.axis_index("seq")

    def at(self, chip, core, z):
        return {"dp": self.base + 2 * chip + core, "seq": z}

    def sibling(self):
        return self.at(self.chip, 1 - self.core, self.z)

    def meet(self):
        barrier = pltpu.get_barrier_semaphore()
        for r in range(4):
            for c in range(2):
                if r + c > 0:
                    pl.semaphore_signal(
                        barrier,
                        inc=1,
                        device_id=self.at(self.chip, (self.core + c) % 2, (self.z + r) % 4),
                        device_id_type=MESH,
                    )
        for r in range(1, 4):
            pl.semaphore_signal(
                barrier,
                inc=1,
                device_id=self.at((self.chip + r) % 4, self.core, self.z),
                device_id_type=MESH,
            )
        return barrier

    def met(self, barrier):
        pl.semaphore_wait(barrier, 10)


def remote(src, dst, send_sem, recv_sem, target):
    return pltpu.make_async_remote_copy(
        src_ref=src,
        dst_ref=dst,
        send_sem=send_sem,
        recv_sem=recv_sem,
        device_id=target,
        device_id_type=MESH,
    )


class Exchange:
    def __init__(self, place, src, dst, sems, row, forward):
        self.place, self.src, self.dst, self.row = place, src, dst, row
        self.local, self.sent, self.got = sems
        z, core = place.z, place.core
        taker = ((z + 1) // 2) % 2
        if forward:
            self.goes = [(2 * core + i, taker) for i in range(2)]
            self.comes = [(core if i == 0 else 3 - core, z // 2) for i in range(2)]
            self.slot = z // 2
        else:
            self.goes = [(core if i == 0 else 3 - core, z // 2) for i in range(2)]
            self.comes = [(2 * core + i, taker) for i in range(2)]
            self.slot = z % 2

    def same(self, spot):
        return (spot[0] == self.place.z) & (spot[1] == self.place.core)

    def far(self, i):
        z, core = self.goes[i]
        return remote(
            self.src.at[i],
            self.dst.at[self.slot],
            self.sent.at[self.row, i],
            self.got.at[self.row, self.slot],
            self.place.at(self.place.chip, core, z),
        )

    def near(self, i):
        return pltpu.make_async_copy(
            self.src.at[i], self.dst.at[self.slot], self.local.at[self.row, i]
        )

    def start(self, i):
        @pl.when(self.same(self.goes[i]))
        def _():
            self.near(i).start()

        @pl.when(jnp.logical_not(self.same(self.goes[i])))
        def _():
            self.far(i).start()

    def arrive(self, i):
        @pl.when(jnp.logical_not(self.same(self.comes[i])))
        def _():
            remote(
                self.dst.at[i],
                self.dst.at[i],
                self.sent.at[self.row, i],
                self.got.at[self.row, i],
                self.place.sibling(),
            ).wait_recv()

    def near_done(self, i):
        @pl.when(self.same(self.goes[i]))
        def _():
            self.near(i).wait()

    def far_done(self, i):
        @pl.when(jnp.logical_not(self.same(self.goes[i])))
        def _():
            self.far(i).wait_send()


class Gather:
    def __init__(self, place, part, full, by_rows, sems, row):
        self.place, self.part, self.full, self.by_rows = place, part, full, by_rows
        self.local, self.sent, self.got = sems
        self.row = row
        self.size = (part.shape[0] if by_rows else part.shape[1]) // 8
        self.mine = 2 * place.chip + place.core

    def block(self, which):
        if self.by_rows:
            return (pl.ds(pl.multiple_of(which * self.size, 16), self.size), slice(None))
        return (slice(None), pl.ds(pl.multiple_of(which * self.size, 128), self.size))

    def window(self, which, quarter):
        return self.full.at[(quarter,) + self.block(which)]

    def copy(self, src, dst, slot, target):
        return remote(src, dst, self.sent.at[self.row, slot], self.got.at[self.row, slot], target)

    def own(self):
        return pltpu.make_async_copy(
            self.part, self.full.at[self.place.z], self.local.at[self.row]
        )

    def over_z(self, r):
        here = self.place
        return self.copy(
            self.part.at[self.block(self.mine)],
            self.window(self.mine, here.z),
            r - 1,
            here.at(here.chip, here.core, (here.z + r) % 4),
        )

    def spread(self, r):
        here = self.place
        ref = self.window(self.mine, (here.z + 4 - r) % 4)
        copies = [
            self.copy(
                ref, ref, 3 * r + s - 1, here.at((here.chip + s) % 4, here.core, here.z)
            )
            for s in range(1, 4)
        ]
        return copies + [self.copy(ref, ref, 11 + r, here.sibling())]

    def hand_on(self, r, s):
        here = self.place
        which = 2 * ((here.chip + 4 - s) % 4) + here.core
        ref = self.window(which, (here.z + 4 - r) % 4)
        return self.copy(ref, ref, 15 + 3 * (r - 1) + s - 1, here.sibling())

    def landed(self, which, r, slot):
        ref = self.window(which, (self.place.z + 4 - r) % 4)
        self.copy(ref, ref, slot, self.place.sibling()).wait_recv()

    def first(self):
        self.own().start()
        for r in range(1, 4):
            self.over_z(r).start()

    def second(self):
        for r in range(1, 4):
            self.landed(self.mine, r, r - 1)
            for item in self.spread(r):
                item.start()

    def third(self):
        for r in range(1, 4):
            for s in range(1, 4):
                which = 2 * ((self.place.chip + 4 - s) % 4) + self.place.core
                self.landed(which, r, 3 * r + s - 1)
                self.hand_on(r, s).start()

    def finish(self):
        chip, other = self.place.chip, 1 - self.place.core
        for r in range(1, 4):
            self.landed(2 * chip + other, r, 11 + r)
            for s in range(1, 4):
                which = 2 * ((chip + 4 - s) % 4) + other
                self.landed(which, r, 15 + 3 * (r - 1) + s - 1)
        self.own().wait()

    def drain(self):
        for r in range(1, 4):
            self.over_z(r).wait_send()
            for item in self.spread(r):
                item.wait_send()
            for s in range(1, 4):
                self.hand_on(r, s).wait_send()


class Scatter:
    def __init__(self, place, grad, out, by_rows, scratch, sems, row):
        self.place, self.grad, self.out, self.by_rows = place, grad, out, by_rows
        self.r0, self.r1, self.r2 = scratch
        self.sent, self.got = sems
        self.row = row
        self.size = (out.shape[0] if by_rows else out.shape[1]) // 8

    def block(self, which):
        if self.by_rows:
            return (pl.ds(pl.multiple_of(which * self.size, 16), self.size), slice(None))
        return (slice(None), pl.ds(pl.multiple_of(which * self.size, 128), self.size))

    def copy(self, src, dst, slot, target):
        return remote(src, dst, self.sent.at[self.row, slot], self.got.at[self.row, slot], target)

    def landed(self, ref, slot):
        self.copy(ref, ref, slot, self.place.sibling()).wait_recv()

    def to_sibling(self, s):
        here = self.place
        which = 2 * ((here.chip + s) % 4) + 1 - here.core
        return self.copy(
            self.grad.at[(slice(None),) + self.block(which)], self.r0.at[s], s, here.sibling()
        )

    def to_chip(self, s):
        here = self.place
        return self.copy(
            self.r0.at[s],
            self.r1.at[s - 1],
            3 + s,
            here.at((here.chip + s) % 4, here.core, here.z),
        )

    def to_z(self, r):
        here = self.place
        return self.copy(
            self.r0.at[0, (here.z + r) % 4],
            self.r2.at[r - 1],
            6 + r,
            here.at(here.chip, here.core, (here.z + r) % 4),
        )

    def spread(self):
        here = self.place
        ref = self.out.at[self.block(2 * here.chip + here.core)]
        copies = [
            self.copy(ref, ref, 9 + s, here.at((here.chip + s) % 4, here.core, here.z))
            for s in range(1, 4)
        ]
        return copies + [self.copy(ref, ref, 13, here.sibling())]

    def hand_on(self, s):
        here = self.place
        ref = self.out.at[self.block(2 * ((here.chip + 4 - s) % 4) + here.core)]
        return self.copy(ref, ref, 13 + s, here.sibling())

    def start(self):
        for s in (1, 2, 3, 0):
            self.to_sibling(s).start()

    def pair(self):
        here = self.place
        for s in (1, 2, 3, 0):
            self.landed(self.r0.at[s], s)
            which = 2 * ((here.chip + s) % 4) + here.core
            mine = self.grad[(slice(None),) + self.block(which)]
            self.r0[s] = (self.r0[s].astype(f32) + mine.astype(f32)).astype(bf16)
            if s > 0:
                self.to_chip(s).start()

    def plane(self):
        for s in range(1, 4):
            self.landed(self.r1.at[s - 1], 3 + s)
        total = self.r0[0].astype(f32)
        for s in range(1, 4):
            total = total + self.r1[s - 1].astype(f32)
        self.r0[0] = total.astype(bf16)
        for r in range(1, 4):
            self.to_z(r).start()

    def line(self):
        for r in range(1, 4):
            self.landed(self.r2.at[r - 1], 6 + r)
        total = self.r0[0, self.place.z].astype(f32)
        for r in range(1, 4):
            total = total + self.r2[r - 1].astype(f32)
        self.out[self.block(2 * self.place.chip + self.place.core)] = total.astype(bf16)
        for item in self.spread():
            item.start()

    def share(self):
        for s in range(1, 4):
            which = 2 * ((self.place.chip + 4 - s) % 4) + self.place.core
            self.landed(self.out.at[self.block(which)], 9 + s)
            self.hand_on(s).start()

    def finish(self):
        chip, other = self.place.chip, 1 - self.place.core
        self.landed(self.out.at[self.block(2 * chip + other)], 13)
        for s in range(1, 4):
            which = 2 * ((chip + 4 - s) % 4) + other
            self.landed(self.out.at[self.block(which)], 13 + s)

    def drain(self):
        for s in range(4):
            self.to_sibling(s).wait_send()
        for s in range(1, 4):
            self.to_chip(s).wait_send()
            self.to_z(s).wait_send()
            self.hand_on(s).wait_send()
        for item in self.spread():
            item.wait_send()


def scatter_scratch(quarters, by_rows):
    _, rows, cols = quarters
    part = (4, rows // 8, cols) if by_rows else (4, rows, cols // 8)
    return [
        pltpu.VMEM((4,) + part, bf16),
        pltpu.VMEM((3,) + part, bf16),
        pltpu.VMEM((3,) + part[1:], bf16),
    ]


def visible(key_start, keys, lows, first_query, own, causal):
    size = lows.shape[1]
    shape = (keys, size - first_query)
    key = lax.broadcasted_iota(jnp.int32, shape, 0) + key_start
    seen = key >= lows[:, first_query:]
    if causal:
        query = lax.broadcasted_iota(jnp.int32, shape, 1) + (own + first_query)
        seen = seen & (key <= query)
    return seen


def flat(values):
    return values.reshape(values.shape[0] * values.shape[1], values.shape[2])


def column(ref, lane):
    tile = lane // 128 * 128
    return flat(ref[:, :, tile : tile + 128]).astype(f32)[:, lane - tile : lane - tile + 1]


def normed(values):
    factor = lax.rsqrt(jnp.mean(values * values, axis=0, keepdims=True) + norm_eps)
    return values * factor, factor


def pack(part, pieces, gain):
    rows = part.shape[0]
    at = 0
    for piece in pieces[:-1]:
        part[:, at : at + piece.shape[1]] = piece[...].astype(bf16)
        at += piece.shape[1]
    last = pieces[-1]
    cut = last.shape[1] // 128 * 128
    part[:, at : at + cut] = last[:, :cut].astype(bf16)
    rest = last.shape[1] - cut
    end = part.shape[1] - at - cut - 128
    gain_col = jnp.broadcast_to(gain[...], (128, rows)).T
    tail = [last[:, cut:], gain_col[:, : 128 - rest]]
    if end > 0:
        tail.append(jnp.zeros((rows, end), f32))
    part[:, at + cut :] = jnp.concatenate(tail, axis=1).astype(bf16)


def layer_kernel(
    tokens, positions, cotangent, turns, balance, projector, combiner, leveler, expander, reducer,
    layer_ref, dx_ref, swide, sdown, sproj,
    xs, dys, q, kv, o, lse, do, dm, out, cos_s, sin_s, low_s, pos, proj, wide, down, give, take,
    wide_a, wide_b, wide_c, down_a, down_b, down_c, proj_a, proj_b, proj_c,
    load, ex_local, ex_sent, ex_got, ga_local, ga_sent, ga_got, sc_sent, sc_got, kv_sent, kv_got,
):
    here = Place()
    core = here.core
    _, model, chunk = xs.shape
    half = chunk // 2
    rows, width = projector.shape
    inner = combiner.shape[1]
    hidden2 = expander.shape[1]
    hidden = hidden2 // 2
    ex = (ex_local, ex_sent, ex_got)
    ga = (ga_local, ga_sent, ga_got)
    sc = (sc_sent, sc_got)
    pos_in = Exchange(here, positions, pos, ex, 0, True)
    x_in = Exchange(here, tokens, xs, ex, 1, True)
    dy_in = Exchange(here, cotangent, dys, ex, 2, True)
    out_back = Exchange(here, out, layer_ref, ex, 3, False)
    dx_back = Exchange(here, out, dx_ref, ex, 4, False)
    down_sum = Scatter(here, down, sdown, True, (down_a, down_b, down_c), sc, 0)
    wide_sum = Scatter(here, wide, swide, False, (wide_a, wide_b, wide_c), sc, 1)
    proj_sum = Scatter(here, proj, sproj, False, (proj_a, proj_b, proj_c), sc, 2)
    barrier = here.meet()
    chunk_of = [core, 3 - core]

    def front(keys, proj_part, wide_part, down_part, stage_p, stage_c, stage_e, stage_r):
        proj_in = Gather(here, proj_part, proj, False, ga, 0)
        wide_in = Gather(here, wide_part, wide, False, ga, 1)
        down_in = Gather(here, down_part, down, True, ga, 2)
        loads = [
            pltpu.make_async_copy(src, dst, load.at[i])
            for i, (src, dst) in enumerate(
                ((projector, stage_p), (combiner, stage_c), (expander, stage_e),
                 (reducer, stage_r))
            )
        ]
        for item in loads:
            item.start()
        loads[0].wait()
        pack(proj_part, [stage_p], balance)
        here.met(barrier)
        proj_in.first()
        for i in range(2):
            pos_in.start(i)
        for i in range(2):
            x_in.start(i)
        for item in loads[1:]:
            item.wait()
        pack(wide_part, [stage_e, stage_c], leveler)
        down_part[...] = stage_r[...].T.astype(bf16)

        for i in range(2):
            pos_in.near_done(i)
        for i in range(2):
            pos_in.arrive(i)
        inverse = jnp.concatenate([turns[...]] * (chunk // 128), axis=1)
        for s in range(2):
            row = jnp.concatenate([pos[s, i : i + 1, :] for i in range(chunk // 128)], axis=1)
            phases = row.astype(f32) * inverse
            cos_s[s] = jnp.cos(phases)
            sin_s[s] = jnp.sin(phases)
            start = chunk_of[s] * chunk
            low_s[s] = lax.broadcasted_iota(jnp.int32, (1, chunk), 1) + start - row

        proj_in.second()
        proj_in.third()
        proj_in.finish()
        gain = column(proj, width)
        w_t = flat(proj[...]).T[:width, :]

        def kv_copy(s):
            ref = kv.at[chunk_of[s]]
            return remote(ref, ref, kv_sent.at[s], kv_got.at[s], here.sibling())

        for i in range(2):
            x_in.near_done(i)
        for s in range(2):
            x_in.arrive(s)
            if s == 1:
                wide_in.first()
                down_in.first()
            n, _ = normed(xs[s].astype(f32))
            a = (n * gain).astype(bf16)
            zs = dot(w_t, a)
            cos = cos_s[s]
            sin = sin_s[s]
            mine = chunk_of[s]

            def rotated(head):
                u1 = zs[head * HEAD_DIM : head * HEAD_DIM + HALF]
                u2 = zs[head * HEAD_DIM + HALF : (head + 1) * HEAD_DIM]
                both = [u1 * cos - u2 * sin, u2 * cos + u1 * sin]
                return jnp.concatenate(both, axis=0).astype(bf16)

            for head in range(KV_HEADS):
                kv[mine, head] = rotated(HEADS + head)
                low = inner + (KV_HEADS + head) * HEAD_DIM
                kv[mine, KV_HEADS + head] = zs[low : low + HEAD_DIM].astype(bf16)
            kv_copy(s).start()
            for head in range(HEADS):
                q[s, head] = rotated(head) * jnp.asarray(0.125, bf16)
        wide_in.second()
        for s in range(2):
            theirs = kv.at[1 - core if s == 0 else 2 + core]
            remote(theirs, theirs, kv_sent.at[s], kv_got.at[s], here.sibling()).wait_recv()
        for s in range(2):
            kv_copy(s).wait_send()
        for c in range(4):
            for g in range(KV_HEADS):
                keys[c, g] = kv[c, g].T

        def outer(step, carry):
            g = step // 2
            s = step % 2
            mine = core + s * (3 - 2 * core)
            lows = low_s[s]
            qs = [q[s, GROUP * g + j] for j in range(GROUP)]

            @pl.when(step == 2)
            def _():
                down_in.second()
                for i in range(2):
                    dy_in.start(i)

            def scores(c, k0, n, q0, causal):
                key_rows = keys[c, g, k0 : k0 + n, :]
                seen = visible(c * chunk + k0, n, lows, q0, mine * chunk, causal)
                raw = [dot(key_rows, each[:, q0:]) for each in qs]
                return [jnp.where(seen, r, NEG) for r in raw]

            def update(c, k0, n, masked, state):
                vals = kv[c, KV_HEADS + g, :, k0 : k0 + n]
                tops = [jnp.max(m, axis=0, keepdims=True) for m in masked]
                if state is not None:
                    tops = [jnp.maximum(old[0], top) for old, top in zip(state, tops)]
                probs = [jnp.exp(m - top) for m, top in zip(masked, tops)]
                lows_ = [p.astype(bf16) for p in probs]
                sums = [jnp.sum(p, axis=0, keepdims=True) for p in probs]
                mixes = [dot(vals, p) for p in lows_]
                if state is None:
                    return tuple(zip(tops, sums, mixes))
                new = []
                for old, top, total, mix in zip(state, tops, sums, mixes):
                    shrink = jnp.exp(old[0] - top)
                    new.append((top, old[1] * shrink + total, old[2] * shrink + mix))
                return tuple(new)

            early = scores(mine, 0, half, 0, True)
            late = scores(mine, half, half, half, True)
            first = update(mine, 0, half, early, None)
            second = update(
                mine, half, half, late, [tuple(part[:, half:] for part in item) for item in first]
            )
            state = tuple(
                tuple(jnp.concatenate([a[:, :half], b], axis=1) for a, b in zip(one, two))
                for one, two in zip(first, second)
            )
            state = lax.fori_loop(
                0,
                mine,
                lambda c, now: update(c, 0, chunk, scores(c, 0, chunk, 0, False), now),
                state,
            )
            for j in range(GROUP):
                top, total, mix = state[j]
                o[s, GROUP * g + j] = (mix / total).astype(bf16)
                lse[s, GROUP * g + j] = top + jnp.log(total)
            return carry

        lax.fori_loop(0, 2 * KV_HEADS, outer, 0)
        for item in (wide_in, down_in):
            item.third()
        for item in (wide_in, down_in):
            item.finish()
        for item in (proj_in, wide_in, down_in):
            item.drain()

    def feed(w_t, down_t, comb_t, act_s, dgu_s, a_s):
        comb0 = hidden2
        gain = column(wide, comb0 + inner)
        size = hidden // 4
        for f in range(8):
            w_t[f * size : (f + 1) * size, :] = flat(wide[:, :, f * size : (f + 1) * size]).T
        for f in range(4):
            down_t[:, f * size : (f + 1) * size] = down[f].T
        comb_t[...] = flat(wide[:, :, comb0 : comb0 + inner]).T
        for i in range(2):
            dy_in.near_done(i)
            dy_in.arrive(i)
        gain_grad = None
        for s in range(2):
            m = xs[s].astype(f32) + dot(comb_t[...], flat(o[s]))
            n, rho = normed(m)
            a = (n * gain).astype(bf16)
            a_s[s] = a
            dy = dys[s]
            for f in range(4):
                low, high = f * size, (f + 1) * size
                g = dot(w_t[low:high, :], a)
                u = dot(w_t[hidden + low : hidden + high, :], a)
                dact = dot(down[f], dy)
                sig = 0.5 * jnp.tanh(0.5 * g) + 0.5
                silu = g * sig
                act_s[s, low:high, :] = (silu * u).astype(bf16)
                dgu_s[s, low:high, :] = (dact * u * (sig + silu * (1.0 - sig))).astype(bf16)
                dgu_s[s, hidden + low : hidden + high, :] = (dact * silu).astype(bf16)
            out[s] = (m + dot(down_t[...], act_s[s])).astype(bf16)
            out_back.start(s)
            da = dot(flat(wide[:, :, :hidden2]), dgu_s[s])
            part = jnp.sum(da * n, axis=1, keepdims=True)
            gain_grad = part if gain_grad is None else gain_grad + part
            dn = da * gain
            dms = dy.astype(f32) + rho * (dn - n * jnp.mean(dn * n, axis=0, keepdims=True))
            dm[s] = dms
            dos = dot(flat(wide[:, :, comb0 : comb0 + inner]), dms.astype(bf16)).astype(bf16)
            do[s] = dos.reshape(HEADS, HEAD_DIM, chunk)
        for f in range(4):
            low, high = f * size, (f + 1) * size
            grad = dot(act_s[0, low:high, :], dys[0], NT) + dot(act_s[1, low:high, :], dys[1], NT)
            down[f] = grad.astype(bf16)
        down_sum.start()

        def wide_grad(f, carry):
            cols = pl.ds(pl.multiple_of(f * size, 128), size)
            grad = dot(a_s[0], dgu_s[0, cols, :], NT) + dot(a_s[1], dgu_s[1, cols, :], NT)
            wide[:, :, cols] = grad.astype(bf16).reshape(4, rows, size)
            return carry

        lax.fori_loop(0, 8, wide_grad, 0)
        grad = dot(flat(o[0]), dm[0].astype(bf16), NT) + dot(flat(o[1]), dm[1].astype(bf16), NT)
        cut = inner // 128 * 128
        end = wide.shape[2] - comb0 - cut
        tail = [
            grad[:, cut:],
            jnp.broadcast_to(gain_grad, (model, 128 - inner + cut)),
            jnp.zeros((model, end - 128), f32),
        ]
        tail = jnp.concatenate(tail, axis=1).astype(bf16).reshape(4, rows, end)
        wide[:, :, comb0 : comb0 + cut] = grad[:, :cut].astype(bf16).reshape(4, rows, cut)
        wide[:, :, comb0 + cut :] = tail
        wide_sum.start()

    def back(keys, values, dkv, dq, dq_now):
        for c in range(4):
            for g in range(KV_HEADS):
                keys[c, g] = kv[c, g].T
                values[c, g] = kv[c, KV_HEADS + g].T
            for g in range(2 * KV_HEADS):
                dkv[c, g] = jnp.zeros((HEAD_DIM, chunk), f32)

        def outer(step, carry):
            g = step // 2
            s = step % 2
            mine = core + s * (3 - 2 * core)
            lows = low_s[s]

            @pl.when(step == 0)
            def _():
                down_sum.pair()

            @pl.when(step == 1)
            def _():
                wide_sum.pair()

            @pl.when(step == 4)
            def _():
                down_sum.plane()

            @pl.when(step == 5)
            def _():
                down_sum.line()

            qs = [q[s, GROUP * g + j] for j in range(GROUP)]
            dos = [do[s, GROUP * g + j] for j in range(GROUP)]
            lses = [lse[s, GROUP * g + j] for j in range(GROUP)]
            deltas = [
                jnp.sum(
                    dos[j].astype(f32) * o[s, GROUP * g + j].astype(f32), axis=0, keepdims=True
                )
                for j in range(GROUP)
            ]

            def block(c, k0, n, q0, causal):
                key_rows = keys[c, g, k0 : k0 + n, :]
                value_rows = values[c, g, k0 : k0 + n, :]
                key_cols = kv[c, g, :, k0 : k0 + n]
                seen = visible(c * chunk + k0, n, lows, q0, mine * chunk, causal)
                raw = [dot(key_rows, each[:, q0:]) for each in qs]
                dps = [dot(value_rows, each[:, q0:]) for each in dos]
                probs = [
                    jnp.exp(jnp.where(seen, r, NEG) - each[:, q0:]) for r, each in zip(raw, lses)
                ]
                lows_ = [p.astype(bf16) for p in probs]
                dss = [
                    (p * (dp - delta[:, q0:])).astype(bf16)
                    for p, dp, delta in zip(probs, dps, deltas)
                ]
                dkv[c, KV_HEADS + g, :, k0 : k0 + n] += dot(
                    jnp.concatenate([each[:, q0:] for each in dos], axis=1),
                    jnp.concatenate(lows_, axis=1),
                    NT,
                )
                dkv[c, g, :, k0 : k0 + n] += dot(
                    jnp.concatenate([each[:, q0:] for each in qs], axis=1),
                    jnp.concatenate(dss, axis=1),
                    NT,
                )
                return [dot(key_cols, ds) for ds in dss]

            early = block(mine, 0, half, 0, True)
            late = block(mine, half, half, half, True)
            for j in range(GROUP):
                dq_now[j] = jnp.concatenate(
                    [early[j][:, :half], early[j][:, half:] + late[j]], axis=1
                )

            def more(c, carry_in):
                extra = block(c, 0, chunk, 0, False)
                for j in range(GROUP):
                    dq_now[j] += extra[j]
                return carry_in

            lax.fori_loop(0, mine, more, 0)
            for j in range(GROUP):
                dq[s, GROUP * g + j] = 0.125 * dq_now[j]
            return carry

        lax.fori_loop(0, 2 * KV_HEADS, outer, 0)

        def give_copy(s):
            return remote(give.at[s], take.at[s], kv_sent.at[s], kv_got.at[s], here.sibling())

        for s in range(2):
            theirs = 1 - core if s == 0 else 2 + core
            give[s] = dkv[theirs].astype(bf16)
            give_copy(s).start()
        for s in range(2):
            out_back.near_done(s)
            out_back.far_done(s)
        gain = column(proj, width)
        w = flat(proj[...])[:, :width]
        grad = None
        gain_grad = None
        for s in range(2):
            cos = cos_s[s]
            sin = sin_s[s]
            mine = chunk_of[s]

            def turned(d):
                d1 = d[:HALF]
                d2 = d[HALF:]
                return jnp.concatenate([d1 * cos + d2 * sin, d2 * cos - d1 * sin], axis=0)

            give_copy(s).wait_recv()
            parts = [turned(dq[s, head]) for head in range(HEADS)]
            full = [dkv[mine, head] + take[s, head].astype(f32) for head in range(2 * KV_HEADS)]
            parts += [turned(full[head]) for head in range(KV_HEADS)]
            parts += full[KV_HEADS:]
            dz = jnp.concatenate([part.astype(bf16) for part in parts], axis=0)
            n, rho = normed(xs[s].astype(f32))
            a = (n * gain).astype(bf16)
            da = dot(w, dz)
            dn = da * gain
            dx = dm[s] + rho * (dn - n * jnp.mean(dn * n, axis=0, keepdims=True))
            out[s] = dx.astype(bf16)
            dx_back.start(s)
            part = dot(a, dz, NT)
            grad = part if grad is None else grad + part
            part = jnp.sum(da * n, axis=1, keepdims=True)
            gain_grad = part if gain_grad is None else gain_grad + part
        gain_cols = jnp.broadcast_to(gain_grad, (model, proj.shape[2] - width))
        full = jnp.concatenate([grad, gain_cols], axis=1).astype(bf16)
        proj[...] = full.reshape(proj.shape)

    pl.run_scoped(
        front,
        pltpu.VMEM((4, KV_HEADS, chunk, HEAD_DIM), bf16),
        pltpu.VMEM(proj.shape[1:], bf16),
        pltpu.VMEM(wide.shape[1:], bf16),
        pltpu.VMEM(down.shape[1:], bf16),
        pltpu.VMEM(projector.shape, f32),
        pltpu.VMEM(combiner.shape, f32),
        pltpu.VMEM(expander.shape, f32),
        pltpu.VMEM(reducer.shape, f32),
    )
    pl.run_scoped(
        feed,
        pltpu.VMEM((hidden2, model), bf16),
        pltpu.VMEM((model, hidden), bf16),
        pltpu.VMEM((model, inner), bf16),
        pltpu.VMEM((2, hidden, chunk), bf16),
        pltpu.VMEM((2, hidden2, chunk), bf16),
        pltpu.VMEM((2, model, chunk), bf16),
    )
    pl.run_scoped(
        back,
        pltpu.VMEM((4, KV_HEADS, chunk, HEAD_DIM), bf16),
        pltpu.VMEM((4, KV_HEADS, chunk, HEAD_DIM), bf16),
        pltpu.VMEM((4, 2 * KV_HEADS, HEAD_DIM, chunk), f32),
        pltpu.VMEM((2, HEADS, HEAD_DIM, chunk), f32),
        pltpu.VMEM((GROUP, HEAD_DIM, chunk), f32),
    )
    proj_sum.start()
    wide_sum.plane()
    proj_sum.pair()
    down_sum.share()
    wide_sum.line()
    proj_sum.plane()
    wide_sum.share()
    proj_sum.line()
    proj_sum.share()
    for item in (down_sum, wide_sum, proj_sum):
        item.finish()
        item.drain()
    for item in (pos_in, x_in, dy_in, dx_back):
        for i in range(2):
            item.far_done(i)
    for i in range(2):
        out_back.arrive(i)
        dx_back.near_done(i)
        dx_back.arrive(i)
    for s in range(2):
        remote(
            give.at[s], take.at[s], kv_sent.at[s], kv_got.at[s], here.sibling()
        ).wait_send()


def layer(tokens, positions, cotangent, weights):
    _, model, chunk = tokens.shape
    rows = weights[1].shape[0]
    hidden = weights[5].shape[1]
    sd = jax.ShapeDtypeStruct
    exponent = np.arange(HALF, dtype=np.float32) * np.float32(2.0 / HEAD_DIM)
    turns = np.power(np.float32(rope_base), -exponent).astype(np.float32)
    turns = jnp.asarray(np.broadcast_to(turns[:, None], (HALF, 128)))
    heads = (2, HEADS, HEAD_DIM, chunk)
    proj, wide, down = (4, rows, 1024), (4, rows, 4096), (4, hidden, model)
    scratch = [
        pltpu.VMEM(tokens.shape, bf16),
        pltpu.VMEM(tokens.shape, bf16),
        pltpu.VMEM(heads, bf16),
        pltpu.VMEM((4, 2 * KV_HEADS, HEAD_DIM, chunk), bf16),
        pltpu.VMEM(heads, bf16),
        pltpu.VMEM((2, HEADS, 1, chunk), f32),
        pltpu.VMEM(heads, bf16),
        pltpu.VMEM(tokens.shape, f32),
        pltpu.VMEM(tokens.shape, bf16),
        pltpu.VMEM((2, HALF, chunk), f32),
        pltpu.VMEM((2, HALF, chunk), f32),
        pltpu.VMEM((2, 1, chunk), jnp.int32),
        pltpu.VMEM((2, chunk // 128, 128), jnp.int32),
        pltpu.VMEM(proj, bf16),
        pltpu.VMEM(wide, bf16),
        pltpu.VMEM(down, bf16),
        pltpu.VMEM((2, 2 * KV_HEADS, HEAD_DIM, chunk), bf16),
        pltpu.VMEM((2, 2 * KV_HEADS, HEAD_DIM, chunk), bf16),
    ]
    for shape, by_rows in ((wide, False), (down, True), (proj, False)):
        scratch += scatter_scratch(shape, by_rows)
    sems = [(4,), (5, 2), (5, 2), (5, 2), (3,), (3, 24), (3, 24), (3, 17), (3, 17), (2,), (2,)]
    scratch += [pltpu.SemaphoreType.DMA(shape) for shape in sems]
    return pl.pallas_call(
        layer_kernel,
        out_shape=[
            sd(tokens.shape, bf16),
            sd(tokens.shape, bf16),
            sd(wide[1:], bf16),
            sd(down[1:], bf16),
            sd(proj[1:], bf16),
        ],
        in_specs=[HBM, VMEM, HBM, VMEM, VMEM, HBM, HBM, VMEM, HBM, HBM],
        out_specs=[HBM, HBM, VMEM, VMEM, VMEM],
        scratch_shapes=scratch,
        compiler_params=pltpu.CompilerParams(
            collective_id=0, has_side_effects=True, vmem_limit_bytes=62 << 20
        ),
    )(tokens, positions.reshape(2, chunk // 128, 128), cotangent, turns, *weights)


def adam_values(master, grad, mean, square, decays):
    mean_new = beta_one * mean + (1.0 - beta_one) * grad
    square_new = beta_two * square + (1.0 - beta_two) * grad * grad
    mean_hat = mean_new / (1.0 - beta_one**STEP)
    square_hat = square_new / (1.0 - beta_two**STEP)
    change = mean_hat / (jnp.sqrt(square_hat) + adam_eps)
    if decays:
        change = change + decay_rate * master
    return master - learn_rate * change, mean_new, square_new


def laid(number, array):
    if number == 5:
        return array.T
    return array[None, :] if array.ndim == 1 else array


def adam_kernel(decay_flags, swide, sdown, sproj, *refs):
    masters, means, squares = refs[:6], refs[6:12], refs[12:18]
    totals, nexts, new_means, new_squares = (refs[18 + 6 * k : 24 + 6 * k] for k in range(4))
    width = masters[1].shape[1]
    inner = masters[2].shape[1]
    hidden2 = masters[4].shape[1]

    def row_of(ref, lane):
        tile = lane // 128 * 128
        return ref[:, tile : tile + 128].astype(f32).T[lane - tile : lane - tile + 1, :]

    grads = (
        lambda: row_of(sproj, width),
        lambda: sproj[:, :width].astype(f32),
        lambda: swide[:, hidden2 : hidden2 + inner].astype(f32),
        lambda: row_of(swide, hidden2 + inner),
        lambda: swide[:, :hidden2].astype(f32),
        lambda: sdown[...].astype(f32).T,
    )
    for i in range(6):
        grad = grads[i]()
        totals[i][...] = grad
        nexts[i][...], new_means[i][...], new_squares[i][...] = adam_values(
            masters[i][...], grad, means[i][...], squares[i][...], decay_flags[i]
        )


def optimize(sums, masters, means, squares):
    decay_flags = (False, True, True, False, True, True)
    arrays = [laid(i % 6, a) for i, a in enumerate(masters + means + squares)]
    shapes = [jax.ShapeDtypeStruct(a.shape, f32) for a in arrays[:6]] * 4
    results = pl.pallas_call(
        functools.partial(adam_kernel, decay_flags),
        out_shape=shapes,
        in_specs=[VMEM] * 21,
        out_specs=[VMEM] * 24,
        compiler_params=pltpu.CompilerParams(vmem_limit_bytes=60 << 20),
    )(*sums, *arrays)
    return tuple(
        r.T if i % 6 == 5 else r.reshape(m.shape)
        for i, (r, m) in enumerate(zip(results, masters * 4))
    )


def on_device(tokens, positions, cotangent, *rest):
    masters, means, squares = rest[:6], rest[6:12], rest[12:18]
    dp_size = lax.axis_size("dp")
    weights = [laid(i, a) for i, a in enumerate(masters)]
    out, dx, *sums = layer(
        jnp.swapaxes(tokens, 1, 2), positions, jnp.swapaxes(cotangent, 1, 2), weights
    )
    if dp_size > 8:
        groups = [[g * 8 + k for g in range(dp_size // 8)] for k in range(8)]
        sums = [lax.psum(part, "dp", axis_index_groups=groups) for part in sums]
    return (jnp.swapaxes(out, 1, 2), jnp.swapaxes(dx, 1, 2)) + optimize(
        sums, masters, means, squares
    )


def solution(mesh):
    vector, matrix = P("seq"), P("seq", None)
    weights = (vector, matrix, matrix, vector, matrix, matrix)
    rows = P("dp", "seq", None)
    return jax.shard_map(
        on_device,
        mesh=mesh,
        in_specs=(rows, P("dp", "seq"), rows) + weights * 3,
        out_specs=(rows, rows) + weights * 4,
        check_vma=False,
    )
```

```python
import functools

import jax
import jax.numpy as jnp
import numpy as np
from jax import lax
from jax.experimental import pallas as pl
from jax.experimental.pallas import tpu as pltpu
from jax.sharding import PartitionSpec as P

HEADS = 9
KV_HEADS = 3
HEAD_DIM = 64
HALF = HEAD_DIM // 2
GROUP = HEADS // KV_HEADS
STEP = 2

norm_eps = 1e-05
rope_base = 100000.0
beta_one = 0.9
beta_two = 0.95
adam_eps = 1e-08
learn_rate = 0.2
decay_rate = 0.1

bf16 = jnp.bfloat16
f32 = jnp.float32
NEG = -1e30
NN = (((1,), (0,)), ((), ()))
NT = (((1,), (1,)), ((), ()))
MESH = pl.DeviceIdType.MESH
VMEM = pl.BlockSpec(memory_space=pltpu.VMEM)
HBM = pl.BlockSpec(memory_space=pl.ANY)


def dot(left, right, dims=NN):
    return lax.dot_general(left, right, dims, preferred_element_type=f32)


class Place:
    def __init__(self):
        dp = lax.axis_index("dp")
        self.base = (dp // 8) * 8
        self.chip = (dp % 8) // 2
        self.core = dp % 2
        self.z = lax.axis_index("seq")

    def at(self, chip, core, z):
        return {"dp": self.base + 2 * chip + core, "seq": z}

    def sibling(self):
        return self.at(self.chip, 1 - self.core, self.z)

    def meet(self):
        barrier = pltpu.get_barrier_semaphore()
        for r in range(4):
            for c in range(2):
                if r + c > 0:
                    pl.semaphore_signal(
                        barrier,
                        inc=1,
                        device_id=self.at(self.chip, (self.core + c) % 2, (self.z + r) % 4),
                        device_id_type=MESH,
                    )
        for r in range(1, 4):
            pl.semaphore_signal(
                barrier,
                inc=1,
                device_id=self.at((self.chip + r) % 4, self.core, self.z),
                device_id_type=MESH,
            )
        return barrier

    def met(self, barrier):
        pl.semaphore_wait(barrier, 10)


def remote(src, dst, send_sem, recv_sem, target):
    return pltpu.make_async_remote_copy(
        src_ref=src,
        dst_ref=dst,
        send_sem=send_sem,
        recv_sem=recv_sem,
        device_id=target,
        device_id_type=MESH,
    )


class Exchange:
    def __init__(self, place, src, dst, sems, row, forward):
        self.place, self.src, self.dst, self.row = place, src, dst, row
        self.local, self.sent, self.got = sems
        z, core = place.z, place.core
        taker = ((z + 1) // 2) % 2
        if forward:
            self.goes = lambda i: (2 * core + i, taker)
            self.comes = lambda i: (core + i * (3 - 2 * core), z // 2)
            self.slot = z // 2
        else:
            self.goes = lambda i: (core + i * (3 - 2 * core), z // 2)
            self.comes = lambda i: (2 * core + i, taker)
            self.slot = z % 2

    def same(self, spot):
        return (spot[0] == self.place.z) & (spot[1] == self.place.core)

    def far(self, i):
        z, core = self.goes(i)
        return remote(
            self.src.at[i],
            self.dst.at[self.slot],
            self.sent.at[self.row, i],
            self.got.at[self.row, self.slot],
            self.place.at(self.place.chip, core, z),
        )

    def near(self, i):
        return pltpu.make_async_copy(
            self.src.at[i], self.dst.at[self.slot], self.local.at[self.row, i]
        )

    def start(self, i):
        @pl.when(self.same(self.goes(i)))
        def _():
            self.near(i).start()

        @pl.when(jnp.logical_not(self.same(self.goes(i))))
        def _():
            self.far(i).start()

    def arrive(self, i):
        @pl.when(jnp.logical_not(self.same(self.comes(i))))
        def _():
            remote(
                self.dst.at[i],
                self.dst.at[i],
                self.sent.at[self.row, i],
                self.got.at[self.row, i],
                self.place.sibling(),
            ).wait_recv()

    def near_done(self, i):
        @pl.when(self.same(self.goes(i)))
        def _():
            self.near(i).wait()

    def far_done(self, i):
        @pl.when(jnp.logical_not(self.same(self.goes(i))))
        def _():
            self.far(i).wait_send()


class Gather:
    def __init__(self, place, part, full, by_rows, sems, row):
        self.place, self.part, self.full, self.by_rows = place, part, full, by_rows
        self.local, self.sent, self.got = sems
        self.row = row
        self.size = full.shape[1 if by_rows else 2] // 8
        self.mine = 2 * place.chip + place.core

    def block(self, which):
        if self.by_rows:
            return (pl.ds(pl.multiple_of(which * self.size, 16), self.size), slice(None))
        return (slice(None), pl.ds(pl.multiple_of(which * self.size, 128), self.size))

    def window(self, which, quarter):
        return self.full.at[(quarter,) + self.block(which)]

    def copy(self, src, dst, slot, target):
        return remote(src, dst, self.sent.at[self.row, slot], self.got.at[self.row, slot], target)

    def own(self):
        return pltpu.make_async_copy(
            self.part, self.full.at[self.place.z], self.local.at[self.row]
        )

    def over_z(self, r):
        here = self.place
        return self.copy(
            self.part.at[self.block(self.mine)],
            self.window(self.mine, here.z),
            r - 1,
            here.at(here.chip, here.core, (here.z + r) % 4),
        )

    def spread(self, r):
        here = self.place
        ref = self.window(self.mine, (here.z + 4 - r) % 4)
        copies = [
            self.copy(
                ref, ref, 3 * r + s - 1, here.at((here.chip + s) % 4, here.core, here.z)
            )
            for s in range(1, 4)
        ]
        return copies + [self.copy(ref, ref, 11 + r, here.sibling())]

    def hand_on(self, r, s):
        here = self.place
        which = 2 * ((here.chip + 4 - s) % 4) + here.core
        ref = self.window(which, (here.z + 4 - r) % 4)
        return self.copy(ref, ref, 15 + 3 * (r - 1) + s - 1, here.sibling())

    def landed(self, which, r, slot):
        ref = self.window(which, (self.place.z + 4 - r) % 4)
        self.copy(ref, ref, slot, self.place.sibling()).wait_recv()

    def first(self):
        self.own().start()
        for r in range(1, 4):
            self.over_z(r).start()

    def second(self):
        for r in range(1, 4):
            self.landed(self.mine, r, r - 1)
            for item in self.spread(r):
                item.start()

    def third(self):
        for r in range(1, 4):
            for s in range(1, 4):
                which = 2 * ((self.place.chip + 4 - s) % 4) + self.place.core
                self.landed(which, r, 3 * r + s - 1)
                self.hand_on(r, s).start()

    def finish(self):
        chip, other = self.place.chip, 1 - self.place.core
        for r in range(1, 4):
            self.landed(2 * chip + other, r, 11 + r)
            for s in range(1, 4):
                which = 2 * ((chip + 4 - s) % 4) + other
                self.landed(which, r, 15 + 3 * (r - 1) + s - 1)

    def drain_part(self):
        for r in range(1, 4):
            self.over_z(r).wait_send()

    def drain(self):
        for r in range(1, 4):
            for item in self.spread(r):
                item.wait_send()
            for s in range(1, 4):
                self.hand_on(r, s).wait_send()


class Scatter:
    def __init__(self, place, grad, out, by_rows, scratch, sems, row):
        self.place, self.grad, self.out, self.by_rows = place, grad, out, by_rows
        self.r0, self.r1, self.r2 = scratch
        self.sent, self.got = sems
        self.row = row
        self.size = (out.shape[0] if by_rows else out.shape[1]) // 8

    def block(self, which):
        if self.by_rows:
            return (pl.ds(pl.multiple_of(which * self.size, 16), self.size), slice(None))
        return (slice(None), pl.ds(pl.multiple_of(which * self.size, 128), self.size))

    def copy(self, src, dst, slot, target):
        return remote(src, dst, self.sent.at[self.row, slot], self.got.at[self.row, slot], target)

    def landed(self, ref, slot):
        self.copy(ref, ref, slot, self.place.sibling()).wait_recv()

    def to_sibling(self, s):
        here = self.place
        which = 2 * ((here.chip + s) % 4) + 1 - here.core
        return self.copy(
            self.grad.at[(slice(None),) + self.block(which)], self.r0.at[s], s, here.sibling()
        )

    def to_chip(self, s):
        here = self.place
        return self.copy(
            self.r0.at[s],
            self.r1.at[s - 1],
            3 + s,
            here.at((here.chip + s) % 4, here.core, here.z),
        )

    def to_z(self, r):
        here = self.place
        return self.copy(
            self.r0.at[0, (here.z + r) % 4],
            self.r2.at[r - 1],
            6 + r,
            here.at(here.chip, here.core, (here.z + r) % 4),
        )

    def spread(self):
        here = self.place
        ref = self.out.at[self.block(2 * here.chip + here.core)]
        copies = [
            self.copy(ref, ref, 9 + s, here.at((here.chip + s) % 4, here.core, here.z))
            for s in range(1, 4)
        ]
        return copies + [self.copy(ref, ref, 13, here.sibling())]

    def hand_on(self, s):
        here = self.place
        ref = self.out.at[self.block(2 * ((here.chip + 4 - s) % 4) + here.core)]
        return self.copy(ref, ref, 13 + s, here.sibling())

    def start(self):
        for s in (1, 2, 3, 0):
            self.to_sibling(s).start()

    def give(self, which):
        @pl.when(which % 2 != self.place.core)
        def _():
            self.to_sibling((which // 2 + 4 - self.place.chip) % 4).start()

    def add(self, s):
        here = self.place
        self.landed(self.r0.at[s], s)
        which = 2 * ((here.chip + s) % 4) + here.core
        mine = self.grad[(slice(None),) + self.block(which)]
        self.r0[s] = (self.r0[s].astype(f32) + mine.astype(f32)).astype(bf16)

    def take(self, which):
        @pl.when(which % 2 == self.place.core)
        def _():
            s = (which // 2 + 4 - self.place.chip) % 4
            self.add(s)

            @pl.when(s > 0)
            def _():
                self.to_chip(s).start()

    def pair(self):
        for s in (1, 2, 3, 0):
            self.add(s)
            if s > 0:
                self.to_chip(s).start()

    def plane(self):
        for s in range(1, 4):
            self.landed(self.r1.at[s - 1], 3 + s)
        total = self.r0[0].astype(f32)
        for s in range(1, 4):
            total = total + self.r1[s - 1].astype(f32)
        self.r0[0] = total.astype(bf16)
        for r in range(1, 4):
            self.to_z(r).start()

    def line(self):
        for r in range(1, 4):
            self.landed(self.r2.at[r - 1], 6 + r)
        total = self.r0[0, self.place.z].astype(f32)
        for r in range(1, 4):
            total = total + self.r2[r - 1].astype(f32)
        self.out[self.block(2 * self.place.chip + self.place.core)] = total.astype(bf16)
        for item in self.spread():
            item.start()

    def share(self):
        for s in range(1, 4):
            which = 2 * ((self.place.chip + 4 - s) % 4) + self.place.core
            self.landed(self.out.at[self.block(which)], 9 + s)
            self.hand_on(s).start()

    def finish(self):
        chip, other = self.place.chip, 1 - self.place.core
        self.landed(self.out.at[self.block(2 * chip + other)], 13)
        for s in range(1, 4):
            which = 2 * ((chip + 4 - s) % 4) + other
            self.landed(self.out.at[self.block(which)], 13 + s)

    def drain(self):
        for s in range(4):
            self.to_sibling(s).wait_send()
        for s in range(1, 4):
            self.to_chip(s).wait_send()
            self.to_z(s).wait_send()
            self.hand_on(s).wait_send()
        for item in self.spread():
            item.wait_send()


def scatter_scratch(quarters, by_rows):
    _, rows, cols = quarters
    part = (4, rows // 8, cols) if by_rows else (4, rows, cols // 8)
    return [
        pltpu.VMEM((4,) + part, bf16),
        pltpu.VMEM((3,) + part, bf16),
        pltpu.VMEM((3,) + part[1:], bf16),
    ]


def visible(key_start, keys, lows, first_query, own, causal):
    size = lows.shape[1]
    shape = (keys, size - first_query)
    key = lax.broadcasted_iota(jnp.int32, shape, 0) + key_start
    seen = key >= lows[:, first_query:]
    if causal:
        query = lax.broadcasted_iota(jnp.int32, shape, 1) + (own + first_query)
        seen = seen & (key <= query)
    return seen


def flat(values):
    return values.reshape(values.shape[0] * values.shape[1], values.shape[2])


def column(ref, lane):
    tile = lane // 128 * 128
    return flat(ref[:, :, tile : tile + 128]).astype(f32)[:, lane - tile : lane - tile + 1]


def normed(values):
    factor = lax.rsqrt(jnp.mean(values * values, axis=0, keepdims=True) + norm_eps)
    return values * factor, factor


def pack(part, pieces, gain):
    rows = part.shape[0]
    at = 0
    for piece in pieces[:-1]:
        part[:, at : at + piece.shape[1]] = piece[...].astype(bf16)
        at += piece.shape[1]
    last = pieces[-1]
    cut = last.shape[1] // 128 * 128
    part[:, at : at + cut] = last[:, :cut].astype(bf16)
    rest = last.shape[1] - cut
    end = part.shape[1] - at - cut - 128
    gain_col = jnp.broadcast_to(gain[...], (128, rows)).T
    tail = [last[:, cut:], gain_col[:, : 128 - rest]]
    if end > 0:
        tail.append(jnp.zeros((rows, end), f32))
    part[:, at + cut :] = jnp.concatenate(tail, axis=1).astype(bf16)


def layer_kernel(
    tokens, positions, cotangent, turns, balance, projector, combiner, leveler, expander, reducer,
    layer_ref, dx_ref, swide, sdown, sproj,
    xs, dys, q, kv, o, lse, do, dm, out, cos_s, sin_s, low_s, pos, proj, wide, down, give, take,
    gwide,
    wide_a, wide_b, wide_c, down_a, down_b, down_c, proj_a, proj_b, proj_c,
    load, ex_local, ex_sent, ex_got, ga_local, ga_sent, ga_got, sc_sent, sc_got, kv_sent, kv_got,
):
    here = Place()
    core = here.core
    _, model, chunk = xs.shape
    half = chunk // 2
    rows, width = projector.shape
    inner = combiner.shape[1]
    hidden2 = expander.shape[1]
    hidden = hidden2 // 2
    ex = (ex_local, ex_sent, ex_got)
    ga = (ga_local, ga_sent, ga_got)
    sc = (sc_sent, sc_got)
    pos_in = Exchange(here, positions, pos, ex, 0, True)
    x_in = Exchange(here, tokens, xs, ex, 1, True)
    dy_in = Exchange(here, cotangent, dys, ex, 2, True)
    out_back = Exchange(here, out, layer_ref, ex, 3, False)
    dx_back = Exchange(here, out, dx_ref, ex, 4, False)
    down_sum = Scatter(here, down, sdown, True, (down_a, down_b, down_c), sc, 0)
    wide_sum = Scatter(here, gwide, swide, False, (wide_a, wide_b, wide_c), sc, 1)
    proj_sum = Scatter(here, proj, sproj, False, (proj_a, proj_b, proj_c), sc, 2)
    barrier = here.meet()
    chunk_of = [core, 3 - core]

    def gathers(proj_part, wide_part, down_part):
        return (
            Gather(here, proj_part, proj, False, ga, 0),
            Gather(here, wide_part, wide, False, ga, 1),
            Gather(here, down_part, down, True, ga, 2),
        )

    def front(keys, proj_part, wide_part, down_part, stage_p, stage_c, stage_e, stage_r):
        proj_in, wide_in, down_in = gathers(proj_part, wide_part, down_part)
        loads = [
            pltpu.make_async_copy(src, dst, load.at[i])
            for i, (src, dst) in enumerate(
                ((projector, stage_p), (combiner, stage_c), (expander, stage_e),
                 (reducer, stage_r))
            )
        ]
        for item in loads:
            item.start()
        loads[0].wait()
        pack(proj_part, [stage_p], balance)
        for item in loads[1:3]:
            item.wait()
        pack(wide_part, [stage_e, stage_c], leveler)
        here.met(barrier)
        proj_in.first()
        for i in range(2):
            pos_in.start(i)
        wide_in.first()
        for i in range(2):
            x_in.start(i)
        loads[3].wait()
        down_part[...] = stage_r[...].T.astype(bf16)
        down_in.first()

        for i in range(2):
            pos_in.near_done(i)
        for i in range(2):
            pos_in.arrive(i)
        inverse = jnp.concatenate([turns[...]] * (chunk // 128), axis=1)
        for s in range(2):
            row = jnp.concatenate([pos[s, i : i + 1, :] for i in range(chunk // 128)], axis=1)
            phases = row.astype(f32) * inverse
            cos_s[s] = jnp.cos(phases)
            sin_s[s] = jnp.sin(phases)
            start = chunk_of[s] * chunk
            low_s[s] = lax.broadcasted_iota(jnp.int32, (1, chunk), 1) + start - row

        proj_in.second()
        proj_in.third()
        proj_in.finish()
        proj_in.own().wait()
        gain = column(proj, width)
        q_t = flat(proj[...]).T[:width, :]
        wide_in.second()

        def kv_copy(s):
            ref = kv.at[core + s * (3 - 2 * core)]
            return remote(ref, ref, kv_sent.at[s], kv_got.at[s], here.sibling())

        for i in range(2):
            x_in.near_done(i)

        def project(k, carry):
            s = k + (here.z // 2) * (1 - 2 * k)
            x_in.arrive(s)

            n, _ = normed(xs[s].astype(f32))
            a = (n * gain).astype(bf16)
            zs = dot(q_t, a)
            cos = cos_s[s]
            sin = sin_s[s]
            mine = core + s * (3 - 2 * core)

            def rotated(head):
                u1 = zs[head * HEAD_DIM : head * HEAD_DIM + HALF]
                u2 = zs[head * HEAD_DIM + HALF : (head + 1) * HEAD_DIM]
                both = [u1 * cos - u2 * sin, u2 * cos + u1 * sin]
                return jnp.concatenate(both, axis=0).astype(bf16)

            for head in range(KV_HEADS):
                kv[mine, head] = rotated(HEADS + head)
                low = inner + (KV_HEADS + head) * HEAD_DIM
                kv[mine, KV_HEADS + head] = zs[low : low + HEAD_DIM].astype(bf16)
            kv_copy(s).start()
            for head in range(HEADS):
                q[s, head] = rotated(head) * jnp.asarray(0.125, bf16)
            return carry

        lax.fori_loop(0, 2, project, 0)
        for s in range(2):
            theirs = kv.at[1 - core if s == 0 else 2 + core]
            remote(theirs, theirs, kv_sent.at[s], kv_got.at[s], here.sibling()).wait_recv()
        for s in range(2):
            kv_copy(s).wait_send()
        for i in range(2):
            dy_in.start(i)
        for c in range(4):
            for g in range(KV_HEADS):
                keys[c, g] = kv[c, g].T

        def outer(step, carry):
            g = step // 2
            s = step % 2
            mine = core + s * (3 - 2 * core)
            lows = low_s[s]
            qs = [q[s, GROUP * g + j] for j in range(GROUP)]

            @pl.when(step == 1)
            def _():
                wide_in.third()

            @pl.when(step == 2)
            def _():
                down_in.second()

            def scores(c, k0, n, q0, causal):
                key_rows = keys[c, g, k0 : k0 + n, :]
                seen = visible(c * chunk + k0, n, lows, q0, mine * chunk, causal)
                raw = [dot(key_rows, each[:, q0:]) for each in qs]
                return [jnp.where(seen, r, NEG) for r in raw]

            def update(c, k0, n, masked, state):
                vals = kv[c, KV_HEADS + g, :, k0 : k0 + n]
                tops = [jnp.max(m, axis=0, keepdims=True) for m in masked]
                if state is not None:
                    tops = [jnp.maximum(old[0], top) for old, top in zip(state, tops)]
                probs = [jnp.exp(m - top) for m, top in zip(masked, tops)]
                lows_ = [p.astype(bf16) for p in probs]
                sums = [jnp.sum(p, axis=0, keepdims=True) for p in probs]
                mixes = [dot(vals, p) for p in lows_]
                if state is None:
                    return tuple(zip(tops, sums, mixes))
                new = []
                for old, top, total, mix in zip(state, tops, sums, mixes):
                    shrink = jnp.exp(old[0] - top)
                    new.append((top, old[1] * shrink + total, old[2] * shrink + mix))
                return tuple(new)

            early = scores(mine, 0, half, 0, True)
            late = scores(mine, half, half, half, True)
            first = update(mine, 0, half, early, None)
            second = update(
                mine, half, half, late, [tuple(part[:, half:] for part in item) for item in first]
            )
            state = tuple(
                tuple(jnp.concatenate([a[:, :half], b], axis=1) for a, b in zip(one, two))
                for one, two in zip(first, second)
            )
            state = lax.fori_loop(
                0,
                mine,
                lambda c, now: update(c, 0, chunk, scores(c, 0, chunk, 0, False), now),
                state,
            )
            for j in range(GROUP):
                top, total, mix = state[j]
                o[s, GROUP * g + j] = (mix / total).astype(bf16)
                lse[s, GROUP * g + j] = top + jnp.log(total)
            return carry

        lax.fori_loop(0, 2 * KV_HEADS, outer, 0)
        down_in.third()
        wide_in.own().wait()
        down_in.own().wait()
        for item in (proj_in, wide_in, down_in):
            item.drain_part()

    def feed(w_t, down_t, comb_t, act_s, dgu_s, a_s):
        proj_in, wide_in, down_in = gathers(None, None, None)
        comb0 = hidden2
        size = hidden // 4
        wide_in.finish()
        gain = column(wide, comb0 + inner)
        comb_t[...] = flat(wide[:, :, comb0 : comb0 + inner]).T
        for f in range(8):
            w_t[f * size : (f + 1) * size, :] = flat(wide[:, :, f * size : (f + 1) * size]).T
        down_in.finish()
        for f in range(4):
            down_t[:, f * size : (f + 1) * size] = down[f].T
        for s in range(2):
            m = xs[s].astype(f32) + dot(comb_t[...], flat(o[s]))
            dm[s] = m
            n, _ = normed(m)
            a = (n * gain).astype(bf16)
            a_s[s] = a
            for f in range(4):
                low, high = f * size, (f + 1) * size
                g = dot(w_t[low:high, :], a)
                u = dot(w_t[hidden + low : hidden + high, :], a)
                sig = 0.5 * jnp.tanh(0.5 * g) + 0.5
                silu = g * sig
                act_s[s, low:high, :] = (silu * u).astype(bf16)
                dgu_s[s, low:high, :] = (u * (sig + silu * (1.0 - sig))).astype(bf16)
                dgu_s[s, hidden + low : hidden + high, :] = silu.astype(bf16)
            out[s] = (m + dot(down_t[...], act_s[s])).astype(bf16)
        gain_grad = None
        for s in range(2):
            dy_in.near_done(s)
            dy_in.arrive(s)
        for s in range(2):
            out_back.start(s)
        for s in range(2):
            dy = dys[s]
            for f in range(4):
                low, high = f * size, (f + 1) * size
                dact = dot(down[f], dy)
                for at in (low, hidden + low):
                    dgu_s[s, at : at + size, :] = (
                        dact * dgu_s[s, at : at + size, :].astype(f32)
                    ).astype(bf16)
        for item in (proj_in, wide_in, down_in):
            item.drain()
        for f in range(4):
            low, high = f * size, (f + 1) * size
            grad = dot(act_s[0, low:high, :], dys[0], NT) + dot(act_s[1, low:high, :], dys[1], NT)
            down[f] = grad.astype(bf16)
        down_sum.start()
        cols_w = wide.shape[2] // 8
        count = hidden2 // cols_w

        def wide_grad(f, carry):
            cols = pl.ds(pl.multiple_of(f * cols_w, 128), cols_w)
            grad = dot(a_s[0], dgu_s[0, cols, :], NT) + dot(a_s[1], dgu_s[1, cols, :], NT)
            gwide[:, :, cols] = grad.astype(bf16).reshape(4, rows, cols_w)
            wide_sum.give(f)

            @pl.when(f == 1)
            def _():
                down_sum.pair()

            @pl.when(f >= 2)
            def _():
                wide_sum.take(f - 2)

            return carry

        lax.fori_loop(0, count, wide_grad, 0)
        for which in range(count - 2, count):
            wide_sum.take(which)
        for s in range(2):
            da = dot(flat(wide[:, :, :hidden2]), dgu_s[s])
            n, rho = normed(dm[s])
            part = jnp.sum(da * n, axis=1, keepdims=True)
            gain_grad = part if gain_grad is None else gain_grad + part
            dn = da * gain
            dms = dys[s].astype(f32) + rho * (dn - n * jnp.mean(dn * n, axis=0, keepdims=True))
            dm[s] = dms
            dos = dot(flat(wide[:, :, comb0 : comb0 + inner]), dms.astype(bf16)).astype(bf16)
            do[s] = dos.reshape(HEADS, HEAD_DIM, chunk)
        grad = dot(flat(o[0]), dm[0].astype(bf16), NT) + dot(flat(o[1]), dm[1].astype(bf16), NT)
        cut = inner // 128 * 128
        end = wide.shape[2] - comb0 - cut
        tail = [
            grad[:, cut:],
            jnp.broadcast_to(gain_grad, (model, 128 - inner + cut)),
            jnp.zeros((model, end - 128), f32),
        ]
        tail = jnp.concatenate(tail, axis=1).astype(bf16).reshape(4, rows, end)
        gwide[:, :, comb0 : comb0 + cut] = grad[:, :cut].astype(bf16).reshape(4, rows, cut)
        gwide[:, :, comb0 + cut :] = tail
        for which in range(count, 8):
            wide_sum.give(which)
        down_sum.plane()

    def back(keys, values, dkv, dq, dq_now):
        for c in range(4):
            for g in range(KV_HEADS):
                keys[c, g] = kv[c, g].T
                values[c, g] = kv[c, KV_HEADS + g].T
            for g in range(2 * KV_HEADS):
                dkv[c, g] = jnp.zeros((HEAD_DIM, chunk), f32)

        def outer(step, carry):
            g = step // 2
            s = step % 2
            mine = core + s * (3 - 2 * core)
            lows = low_s[s]

            @pl.when(step == 0)
            def _():
                for which in range(6, 8):
                    wide_sum.take(which)

            @pl.when(step == 2)
            def _():
                down_sum.line()

            @pl.when(step == 4)
            def _():
                down_sum.share()
                wide_sum.plane()

            qs = [q[s, GROUP * g + j] for j in range(GROUP)]
            dos = [do[s, GROUP * g + j] for j in range(GROUP)]
            lses = [lse[s, GROUP * g + j] for j in range(GROUP)]
            deltas = [
                jnp.sum(
                    dos[j].astype(f32) * o[s, GROUP * g + j].astype(f32), axis=0, keepdims=True
                )
                for j in range(GROUP)
            ]

            def block(c, k0, n, q0, causal):
                key_rows = keys[c, g, k0 : k0 + n, :]
                value_rows = values[c, g, k0 : k0 + n, :]
                key_cols = kv[c, g, :, k0 : k0 + n]
                seen = visible(c * chunk + k0, n, lows, q0, mine * chunk, causal)
                raw = [dot(key_rows, each[:, q0:]) for each in qs]
                dps = [dot(value_rows, each[:, q0:]) for each in dos]
                probs = [
                    jnp.exp(jnp.where(seen, r, NEG) - each[:, q0:]) for r, each in zip(raw, lses)
                ]
                lows_ = [p.astype(bf16) for p in probs]
                dss = [
                    (p * (dp - delta[:, q0:])).astype(bf16)
                    for p, dp, delta in zip(probs, dps, deltas)
                ]
                dkv[c, KV_HEADS + g, :, k0 : k0 + n] += dot(
                    jnp.concatenate([each[:, q0:] for each in dos], axis=1),
                    jnp.concatenate(lows_, axis=1),
                    NT,
                )
                dkv[c, g, :, k0 : k0 + n] += dot(
                    jnp.concatenate([each[:, q0:] for each in qs], axis=1),
                    jnp.concatenate(dss, axis=1),
                    NT,
                )
                return [dot(key_cols, ds) for ds in dss]

            early = block(mine, 0, half, 0, True)
            late = block(mine, half, half, half, True)
            for j in range(GROUP):
                dq_now[j] = jnp.concatenate(
                    [early[j][:, :half], early[j][:, half:] + late[j]], axis=1
                )

            def more(c, carry_in):
                extra = block(c, 0, chunk, 0, False)
                for j in range(GROUP):
                    dq_now[j] += extra[j]
                return carry_in

            lax.fori_loop(0, mine, more, 0)
            for j in range(GROUP):
                dq[s, GROUP * g + j] = 0.125 * dq_now[j]
            return carry

        lax.fori_loop(0, 2 * KV_HEADS, outer, 0)

        def give_copy(s):
            return remote(give.at[s], take.at[s], kv_sent.at[s], kv_got.at[s], here.sibling())

        for s in range(2):
            theirs = 1 - core if s == 0 else 2 + core
            give[s] = dkv[theirs].astype(bf16)
            give_copy(s).start()
        wide_sum.line()
        for s in range(2):
            out_back.near_done(s)
            out_back.far_done(s)
        gain = column(proj, width)
        w = flat(proj[...])[:, :width]
        grad = None
        gain_grad = None
        for s in range(2):
            cos = cos_s[s]
            sin = sin_s[s]
            mine = chunk_of[s]

            def turned(d):
                d1 = d[:HALF]
                d2 = d[HALF:]
                return jnp.concatenate([d1 * cos + d2 * sin, d2 * cos - d1 * sin], axis=0)

            give_copy(s).wait_recv()
            parts = [turned(dq[s, head]) for head in range(HEADS)]
            full = [dkv[mine, head] + take[s, head].astype(f32) for head in range(2 * KV_HEADS)]
            parts += [turned(full[head]) for head in range(KV_HEADS)]
            parts += full[KV_HEADS:]
            dz = jnp.concatenate([part.astype(bf16) for part in parts], axis=0)
            n, rho = normed(xs[s].astype(f32))
            a = (n * gain).astype(bf16)
            da = dot(w, dz)
            dn = da * gain
            dx = dm[s] + rho * (dn - n * jnp.mean(dn * n, axis=0, keepdims=True))
            out[s] = dx.astype(bf16)
            dx_back.start(s)
            part = dot(a, dz, NT)
            grad = part if grad is None else grad + part
            part = jnp.sum(da * n, axis=1, keepdims=True)
            gain_grad = part if gain_grad is None else gain_grad + part
        gain_cols = jnp.broadcast_to(gain_grad, (model, proj.shape[2] - width))
        full = jnp.concatenate([grad, gain_cols], axis=1).astype(bf16)
        proj[...] = full.reshape(proj.shape)

    pl.run_scoped(
        front,
        pltpu.VMEM((4, KV_HEADS, chunk, HEAD_DIM), bf16),
        pltpu.VMEM(proj.shape[1:], bf16),
        pltpu.VMEM(wide.shape[1:], bf16),
        pltpu.VMEM(down.shape[1:], bf16),
        pltpu.VMEM(projector.shape, f32),
        pltpu.VMEM(combiner.shape, f32),
        pltpu.VMEM(expander.shape, f32),
        pltpu.VMEM(reducer.shape, f32),
    )
    pl.run_scoped(
        feed,
        pltpu.VMEM((hidden2, model), bf16),
        pltpu.VMEM((model, hidden), bf16),
        pltpu.VMEM((model, inner), bf16),
        pltpu.VMEM((2, hidden, chunk), bf16),
        pltpu.VMEM((2, hidden2, chunk), bf16),
        pltpu.VMEM((2, model, chunk), bf16),
    )
    pl.run_scoped(
        back,
        pltpu.VMEM((4, KV_HEADS, chunk, HEAD_DIM), bf16),
        pltpu.VMEM((4, KV_HEADS, chunk, HEAD_DIM), bf16),
        pltpu.VMEM((4, 2 * KV_HEADS, HEAD_DIM, chunk), f32),
        pltpu.VMEM((2, HEADS, HEAD_DIM, chunk), f32),
        pltpu.VMEM((GROUP, HEAD_DIM, chunk), f32),
    )
    proj_sum.start()
    proj_sum.pair()
    wide_sum.share()
    proj_sum.plane()
    proj_sum.line()
    proj_sum.share()
    for item in (down_sum, wide_sum, proj_sum):
        item.finish()
        item.drain()
    for item in (pos_in, x_in, dy_in, dx_back):
        for i in range(2):
            item.far_done(i)
    for i in range(2):
        out_back.arrive(i)
        dx_back.near_done(i)
        dx_back.arrive(i)
    for s in range(2):
        remote(
            give.at[s], take.at[s], kv_sent.at[s], kv_got.at[s], here.sibling()
        ).wait_send()


def layer(tokens, positions, cotangent, weights):
    _, model, chunk = tokens.shape
    rows = weights[1].shape[0]
    hidden = weights[5].shape[1]
    sd = jax.ShapeDtypeStruct
    exponent = np.arange(HALF, dtype=np.float32) * np.float32(2.0 / HEAD_DIM)
    turns = np.power(np.float32(rope_base), -exponent).astype(np.float32)
    turns = jnp.asarray(np.broadcast_to(turns[:, None], (HALF, 128)))
    heads = (2, HEADS, HEAD_DIM, chunk)
    proj, wide, down = (4, rows, 1024), (4, rows, 4096), (4, hidden, model)
    scratch = [
        pltpu.VMEM(tokens.shape, bf16),
        pltpu.VMEM(tokens.shape, bf16),
        pltpu.VMEM(heads, bf16),
        pltpu.VMEM((4, 2 * KV_HEADS, HEAD_DIM, chunk), bf16),
        pltpu.VMEM(heads, bf16),
        pltpu.VMEM((2, HEADS, 1, chunk), f32),
        pltpu.VMEM(heads, bf16),
        pltpu.VMEM(tokens.shape, f32),
        pltpu.VMEM(tokens.shape, bf16),
        pltpu.VMEM((2, HALF, chunk), f32),
        pltpu.VMEM((2, HALF, chunk), f32),
        pltpu.VMEM((2, 1, chunk), jnp.int32),
        pltpu.VMEM((2, chunk // 128, 128), jnp.int32),
        pltpu.VMEM(proj, bf16),
        pltpu.VMEM(wide, bf16),
        pltpu.VMEM(down, bf16),
        pltpu.VMEM((2, 2 * KV_HEADS, HEAD_DIM, chunk), bf16),
        pltpu.VMEM((2, 2 * KV_HEADS, HEAD_DIM, chunk), bf16),
        pltpu.VMEM(wide, bf16),
    ]
    for shape, by_rows in ((wide, False), (down, True), (proj, False)):
        scratch += scatter_scratch(shape, by_rows)
    sems = [(4,), (5, 2), (5, 2), (5, 2), (3,), (3, 24), (3, 24), (3, 17), (3, 17), (2,), (2,)]
    scratch += [pltpu.SemaphoreType.DMA(shape) for shape in sems]
    return pl.pallas_call(
        layer_kernel,
        out_shape=[
            sd(tokens.shape, bf16),
            sd(tokens.shape, bf16),
            sd(wide[1:], bf16),
            sd(down[1:], bf16),
            sd(proj[1:], bf16),
        ],
        in_specs=[HBM, VMEM, HBM, VMEM, VMEM, HBM, HBM, VMEM, HBM, HBM],
        out_specs=[HBM, HBM, VMEM, VMEM, VMEM],
        scratch_shapes=scratch,
        compiler_params=pltpu.CompilerParams(
            collective_id=0, has_side_effects=True, vmem_limit_bytes=62 << 20
        ),
    )(tokens, positions.reshape(2, chunk // 128, 128), cotangent, turns, *weights)


def adam_values(master, grad, mean, square, decays):
    mean_new = beta_one * mean + (1.0 - beta_one) * grad
    square_new = beta_two * square + (1.0 - beta_two) * grad * grad
    mean_hat = mean_new / (1.0 - beta_one**STEP)
    square_hat = square_new / (1.0 - beta_two**STEP)
    change = mean_hat / (jnp.sqrt(square_hat) + adam_eps)
    if decays:
        change = change + decay_rate * master
    return master - learn_rate * change, mean_new, square_new


def laid(number, array):
    if number == 5:
        return array.T
    return array[None, :] if array.ndim == 1 else array


def adam_kernel(decay_flags, swide, sdown, sproj, *refs):
    masters, means, squares = refs[:6], refs[6:12], refs[12:18]
    totals, nexts, new_means, new_squares = (refs[20 + 6 * k : 26 + 6 * k] for k in range(4))
    width = masters[1].shape[1]
    inner = masters[2].shape[1]
    hidden2 = masters[4].shape[1]

    def row_of(ref, lane):
        tile = lane // 128 * 128
        return ref[:, tile : tile + 128].astype(f32).T[lane - tile : lane - tile + 1, :]

    grads = (
        lambda: row_of(sproj, width),
        lambda: sproj[:, :width].astype(f32),
        lambda: swide[:, hidden2 : hidden2 + inner].astype(f32),
        lambda: row_of(swide, hidden2 + inner),
        lambda: swide[:, :hidden2].astype(f32),
        lambda: sdown[...].astype(f32).T,
    )
    for i in range(6):
        grad = grads[i]()
        totals[i][...] = grad
        nexts[i][...], new_means[i][...], new_squares[i][...] = adam_values(
            masters[i][...], grad, means[i][...], squares[i][...], decay_flags[i]
        )


def optimize(sums, masters, means, squares, passed):
    decay_flags = (False, True, True, False, True, True)
    arrays = [laid(i % 6, a) for i, a in enumerate(masters + means + squares)]
    shapes = [jax.ShapeDtypeStruct(a.shape, f32) for a in arrays[:6]] * 4
    results = pl.pallas_call(
        functools.partial(adam_kernel, decay_flags),
        out_shape=shapes + [jax.ShapeDtypeStruct(a.shape, a.dtype) for a in passed],
        in_specs=[VMEM] * 21 + [HBM] * 2,
        out_specs=[VMEM] * 24 + [HBM] * 2,
        input_output_aliases={21: 24, 22: 25},
        compiler_params=pltpu.CompilerParams(vmem_limit_bytes=60 << 20),
    )(*sums, *arrays, *passed)
    return tuple(jnp.swapaxes(r, 1, 2) for r in results[24:]) + tuple(
        r.T if i % 6 == 5 else r.reshape(m.shape)
        for i, (r, m) in enumerate(zip(results, masters * 4))
    )


def on_device(tokens, positions, cotangent, *rest):
    masters, means, squares = rest[:6], rest[6:12], rest[12:18]
    dp_size = lax.axis_size("dp")
    weights = [laid(i, a) for i, a in enumerate(masters)]
    out, dx, *sums = layer(
        jnp.swapaxes(tokens, 1, 2), positions, jnp.swapaxes(cotangent, 1, 2), weights
    )
    if dp_size > 8:
        groups = [[g * 8 + k for g in range(dp_size // 8)] for k in range(8)]
        sums = [lax.psum(part, "dp", axis_index_groups=groups) for part in sums]
    return optimize(sums, masters, means, squares, (out, dx))


def solution(mesh):
    vector, matrix = P("seq"), P("seq", None)
    weights = (vector, matrix, matrix, vector, matrix, matrix)
    rows = P("dp", "seq", None)
    return jax.shard_map(
        on_device,
        mesh=mesh,
        in_specs=(rows, P("dp", "seq"), rows) + weights * 3,
        out_specs=(rows, rows) + weights * 4,
        check_vma=False,
    )
```
